512 devices in a mesh: fsdp: 32 (over z, core), tensor: 16 (over x, y).
Axes of the slice: x: 4, y: 4, z: 16, core: 2. Of those that a mesh axis runs over, the one named last changes fastest.
Arguments:
- weights: bfloat16 [8192, 14336], P('fsdp', 'tensor'), may hold values from -6 to 6
- momentum: float32 [8192, 14336], P('fsdp', 'tensor'), may hold values from -40 to 40
- gradient: bfloat16 [8192, 14336], P('fsdp', 'tensor'), may hold values from -20 to 20
- warm_basis: float32 [512, 14336], P('fsdp', 'tensor'), may hold values from -6 to 6
Outputs:
- new_weights: bfloat16 [8192, 14336], P('fsdp', 'tensor')
- new_momentum: float32 [8192, 14336], P('fsdp', 'tensor')
- new_basis: float32 [512, 14336], P('fsdp', 'tensor')
The draws below stay inside these ranges and needn't reach their ends.
All inputs are finite; a program needn't handle non-finite values.
Results may differ from the reference program's by a relative error of at most 0.001.
Values sent between devices are 32-bit elements; how exact they have to be, the bound alone decides.
No kernel may reach another device: no remote copies, remote signals or barrier semaphores. Data moves between devices by JAX's collectives and lax.ppermute only.
A program may use at most 64 MiB of HBM per device.

```python
import math
import jax
import jax.numpy as jnp
from jax import lax

D = 8192
FF = 14336
RANK = 512


def column_scales(key):
    where = jnp.arange(FF, dtype=jnp.float32) / FF
    jitter = jax.random.uniform(key, (FF,), jnp.float32, -0.6, 0.6)
    return jnp.exp(jnp.log(3.0) * (where - 0.5) + jitter)


def draw_momentum(key, part):
    columns = column_scales(key)
    key = jax.random.fold_in(key, 3)
    row_key, noise_key = jax.random.split(key)
    row_scales = jnp.exp(jax.random.uniform(row_key, (D,), jnp.float32, -0.7, 0.7))
    noise = jnp.clip(jax.random.normal(noise_key, (D, FF), jnp.float32), -6.0, 6.0)
    return noise * row_scales[:, None] * columns[None, :]


def draw_gradient(key, part):
    columns = column_scales(key)
    key = jax.random.fold_in(key, 5)
    row_key, noise_key = jax.random.split(key)
    row_scales = 0.5 * jnp.exp(jax.random.uniform(row_key, (D,), jnp.float32, -0.7, 0.7))
    noise = jnp.clip(jax.random.normal(noise_key, (D, FF), jnp.float32), -6.0, 6.0)
    return (noise * row_scales[:, None] * columns[None, :]).astype(jnp.bfloat16)


def level_of(stream_key, shape, cuts, least, high):
    loudness, own = 1.0, jax.random.fold_in(stream_key, 6)
    for axis_at, shards_of in cuts:
        draws = jnp.exp(jax.random.uniform(jax.random.fold_in(own, axis_at), (shards_of,), jnp.float32, least / len(cuts), high / len(cuts)))
        loudness = loudness * jnp.repeat(draws, shape[axis_at] // shards_of).reshape([-1 if axis == axis_at else 1 for axis in range(len(shape))])
    return loudness


def bell_draw(key, shape, width, limit, pieces=(), kind=jnp.bfloat16):
    array = width * jax.random.normal(key, shape, jnp.float32)
    if pieces:
        array = array * level_of(key, shape, pieces, -0.22, 0.18)
    return jnp.clip(array, -limit, limit).astype(kind)


def setup_inputs(seed: int = 0) -> dict:
    key_list = jax.random.split(jax.random.key(seed), 5)
    return {
        "weights": bell_draw(key_list[0], (D, FF), 1.0, 6.0, ((0, 32), (1, 16))),
        "momentum": draw_momentum(jax.random.fold_in(key_list[4], 71), 0),
        "gradient": draw_gradient(jax.random.fold_in(key_list[4], 71), 0),
        "warm_basis": bell_draw(key_list[3], (RANK, FF), 1.0, 6.0, ((0, 32), (1, 16)), jnp.float32),
    }


momentum_decay = 0.95
step_size = 2.0
epsilon = 1e-06

def reference(weights, momentum, gradient, warm_basis):
    highest = lax.Precision.HIGHEST
    blended = momentum + gradient.astype(jnp.float32)
    projected = lax.dot_general(blended.astype(jnp.float32), warm_basis.astype(jnp.float32), (((1,), (1,)), ((), ())), precision=highest, preferred_element_type=jnp.float32)
    gram = lax.dot_general(projected.astype(jnp.float32), projected.astype(jnp.float32), (((0,), (0,)), ((), ())), precision=highest, preferred_element_type=jnp.float32)
    factor = jnp.linalg.cholesky(gram)
    orthonormal = lax.linalg.triangular_solve(factor, projected, left_side=False, lower=True, transpose_a=True)
    coefficients = lax.dot_general(orthonormal.astype(jnp.float32), blended.astype(jnp.float32), (((0,), (0,)), ((), ())), precision=highest, preferred_element_type=jnp.float32)
    mean_square = lax.optimization_barrier(jnp.sum(coefficients * coefficients, axis=1)) / FF
    new_basis = coefficients * lax.rsqrt(mean_square + epsilon)[:, None]
    feedback = jnp.dot(orthonormal.astype(jnp.float32), coefficients.astype(jnp.float32), precision=highest, preferred_element_type=jnp.float32)
    update = jnp.dot(orthonormal.astype(jnp.float32), new_basis.astype(jnp.float32), precision=highest, preferred_element_type=jnp.float32)
    new_momentum = blended - (1.0 - momentum_decay) * feedback
    new_weights = (weights.astype(jnp.float32) - step_size * math.sqrt(D / FF) * update).astype(jnp.bfloat16)
    return (new_weights, new_momentum, new_basis)
```

```python
import math

import jax
import jax.numpy as jnp
from jax import lax
from jax.sharding import Mesh, PartitionSpec as P

D = 8192
FF = 14336

momentum_decay = 0.95
step_size = 2.0
epsilon = 1e-06

PLANE = ("core", "x", "y")
COLUMN_BLOCKS = ("x", "y")
SWAP = [(0, 1), (1, 0)]


def dot(left_side, right_side, contract_left, contract_right, precision=lax.Precision.HIGHEST):
    return lax.dot_general(
        left_side,
        right_side,
        (((contract_left,), (contract_right,)), ((), ())),
        precision=precision,
        preferred_element_type=jnp.float32,
    )


def exchange(array, axes):
    return lax.all_to_all(array, axes, 0, 0, tiled=True)


def spread(array, axes, count):
    return exchange(
        jnp.broadcast_to(array[None], (count,) + array.shape).reshape(
            (count * array.shape[0],) + array.shape[1:]
        ),
        axes,
    )


def inverse_factor(gram):
    factor = jnp.linalg.cholesky(gram)
    return lax.linalg.triangular_solve(
        factor, jnp.eye(gram.shape[0], dtype=jnp.float32), left_side=True, lower=True
    )


def on_device(weights, momentum, gradient, warm_basis):
    rows, columns = momentum.shape
    owned = warm_basis.shape[0]
    depth = lax.axis_size("z")
    plane = lax.axis_size(PLANE)
    blocks = lax.axis_size(COLUMN_BLOCKS)
    rank = owned * depth * 2
    core = lax.axis_index("core")
    place = lax.axis_index("z")

    blended = momentum + gradient.astype(jnp.float32)
    partner = lax.ppermute(blended, "core", SWAP)
    basis = lax.all_gather(warm_basis, "z", axis=0, tiled=True)
    mine = dot(blended, basis, 1, 1)
    theirs = dot(partner, basis, 1, 1)
    partial = jnp.where(
        core == 0, jnp.stack([mine, theirs]), jnp.stack([theirs, mine])
    ).reshape(2 * rows, rank // 2)
    pieces = exchange(partial, PLANE).reshape(2, blocks, 2 * rows // plane, depth, owned)
    part = jnp.sum(pieces, axis=1).transpose(1, 2, 0, 3).reshape(2 * rows // plane, rank)
    projected = spread(part, PLANE, plane)

    share = rank // plane
    mine_at = lax.axis_index(PLANE) * share
    gram_part = dot(lax.dynamic_slice_in_dim(projected, mine_at, share, 1), projected, 0, 0)
    gram_row = jnp.sum(exchange(gram_part, "z").reshape(depth, share // depth, rank), axis=0)
    gram_share = spread(gram_row, "z", depth)
    gram = spread(gram_share, PLANE, plane)

    half = lax.dynamic_slice_in_dim(projected, core * (rank // 2), rank // 2, 1)
    own_rows = lax.dynamic_slice_in_dim(half, core * rows, rows, 0)
    partner_rows = lax.dynamic_slice_in_dim(half, (1 - core) * rows, rows, 0)
    moved = dot(own_rows, blended, 0, 0) + dot(partner_rows, partner, 0, 0)
    moved = lax.psum_scatter(moved, "z", scatter_dimension=0, tiled=True)
    moved = lax.all_gather(moved, "z", axis=0, tiled=True)
    moved = spread(moved, "core", 2)

    inverse = inverse_factor(gram)
    own_projected = lax.dynamic_slice_in_dim(projected, core * rows, rows, 0)
    orthonormal = dot(own_projected, inverse, 1, 1)
    coefficients = dot(inverse, moved, 1, 0)
    energy = jnp.sum(coefficients * coefficients, axis=1).reshape(rank // 128, 128)
    energy = jnp.sum(
        spread(energy, COLUMN_BLOCKS, blocks).reshape(blocks, rank // 128, 128), axis=0
    ).reshape(rank)
    scale = lax.rsqrt(energy / FF + epsilon)
    feedback = dot(orthonormal, coefficients, 1, 0)
    new_momentum = blended - (1.0 - momentum_decay) * feedback
    update = dot(orthonormal * scale[None, :], coefficients, 1, 0)
    first = (place * 2 + core) * owned
    new_basis = (
        lax.dynamic_slice_in_dim(coefficients, first, owned, 0)
        * lax.dynamic_slice_in_dim(scale, first, owned, 0)[:, None]
    )
    new_weights = (weights.astype(jnp.float32) - step_size * math.sqrt(D / FF) * update).astype(
        jnp.bfloat16
    )
    return (new_weights, new_momentum, new_basis)


def solution(mesh):
    devices = mesh.devices
    split = Mesh(
        devices.reshape(devices.shape[0] // 2, 2, 4, devices.shape[1] // 4),
        ("z", "core", "x", "y"),
    )
    spec = P(("z", "core"), ("x", "y"))
    return jax.shard_map(
        on_device, mesh=split, in_specs=(spec,) * 4, out_specs=(spec,) * 3, check_vma=False
    )
```

```python
import math

import jax
import jax.numpy as jnp
from jax import lax
from jax.experimental import pallas as pl
from jax.experimental.pallas import tpu as pltpu
from jax.sharding import Mesh, PartitionSpec as P

D = 8192
FF = 14336

momentum_decay = 0.95
step_size = 2.0
epsilon = 1e-06

PLANE = ("core", "x", "y")
COLUMN_BLOCKS = ("x", "y")
SWAP = [(0, 1), (1, 0)]


def dot(left_side, right_side, contract_left, contract_right, precision=lax.Precision.HIGHEST):
    return lax.dot_general(
        left_side,
        right_side,
        (((contract_left,), (contract_right,)), ((), ())),
        precision=precision,
        preferred_element_type=jnp.float32,
    )


def exchange(array, axes):
    return lax.all_to_all(array, axes, 0, 0, tiled=True)


def spread(array, axes, count):
    return exchange(
        jnp.broadcast_to(array[None], (count,) + array.shape).reshape(
            (count * array.shape[0],) + array.shape[1:]
        ),
        axes,
    )


SUB = 8
TILE = 128


def factor_step(work, wide, at):
    lane = lax.broadcasted_iota(jnp.int32,(SUB,TILE),1)
    sub = lax.broadcasted_iota(jnp.int32,(SUB,TILE),0)
    own = (lane>=at)&(lane<at+SUB)
    block = work[at:at+SUB,:]
    for j in range(SUB):
        wide[j] = jnp.broadcast_to(block[:,at+j:at+j+1],(SUB,TILE))
    work[at:at+SUB,:] = jnp.where(own, jnp.where(lane-at==sub,1.0,0.0), block)
    spread = lambda ref_row: jnp.broadcast_to(ref_row,(SUB,TILE))
    gram = [[spread(wide[j,i:i+1,:]) for j in range(i+1)] for i in range(SUB)]
    low = [[None]*SUB for _ in range(SUB)]
    inv = [None]*SUB
    rows = [None]*SUB
    for j in range(SUB):
        inv[j] = lax.rsqrt(gram[j][j])
        for i in range(j+1,SUB):
            low[i][j] = gram[i][j]*inv[j]
        for i in range(j+1,SUB):
            for m in range(j+1,i+1):
                gram[i][m] = gram[i][m]-low[i][j]*low[m][j]
        row = spread(work[at+j:at+j+1,:])
        for m in range(j):
            row = row - low[j][m]*rows[m]
        rows[j] = row*inv[j]
    out = rows[SUB-1]
    for i in range(SUB-1):
        out = jnp.where(sub==i, rows[i], out)
    work[at:at+SUB,:] = out
    nxt = at+SUB
    if nxt < TILE:
        block = work[nxt:nxt+SUB,:]
        left=[]
        total = jnp.where(own,0.0,block)
        for j in range(SUB):
            col = jnp.broadcast_to(block[:,at+j:at+j+1],(SUB,TILE))
            for m in range(j):
                col = col - left[m]*low[j][m]
            left.append(col*inv[j])
            total = total - left[j]*rows[j]
        work[nxt:nxt+SUB,:] = total
    far = nxt+SUB
    if far < TILE:
        prod = dot(out,out,0,0)
        rest = work[far:,:]
        lanes = lax.broadcasted_iota(jnp.int32,rest.shape,1)
        work[far:,:] = jnp.where((lanes>=at)&(lanes<at+SUB),0.0,rest) - prod[far:,:]


def inverse_factor_kernel(gram_ref, out_ref, work, wide):
    n = gram_ref.shape[0]; tiles = n//TILE
    out_ref[...] = gram_ref[...]
    def panel(p, carry):
        at = pl.multiple_of(p*TILE,TILE)
        work[...] = out_ref[pl.ds(at,TILE),pl.ds(at,TILE)]
        for k in range(TILE//SUB):
            factor_step(work, wide.at[k%2], k*SUB)
        r = lax.broadcasted_iota(jnp.int32,(TILE,TILE),0); c = lax.broadcasted_iota(jnp.int32,(TILE,TILE),1)
        inverse = jnp.where(r>=c, work[...], 0.0)
        out_ref[pl.ds(at,TILE),pl.ds(at,TILE)] = jnp.where(r==c,1.0,0.0)
        new = dot(inverse, out_ref[pl.ds(at,TILE),:],1,0)
        out_ref[pl.ds(at,TILE),:] = new
        for q in range(1,tiles):
            @pl.when(q>p)
            def _():
                out_ref[q*TILE:(q+1)*TILE,pl.ds(at,TILE)] = jnp.zeros((TILE,TILE),jnp.float32)
                out_ref[q*TILE:(q+1)*TILE,:] = out_ref[q*TILE:(q+1)*TILE,:] - dot(
                    new[:,q*TILE:(q+1)*TILE],new,0,0
                )
        return carry
    lax.fori_loop(0,tiles,panel,0)
    for q in range(tiles-1):
        out_ref[q*TILE:(q+1)*TILE,(q+1)*TILE:] = jnp.zeros((TILE,n-(q+1)*TILE),jnp.float32)


def inverse_factor(gram):
    size = gram.shape[0]
    return pl.pallas_call(
        inverse_factor_kernel,
        out_shape=jax.ShapeDtypeStruct((size, size), jnp.float32),
        in_specs=[pl.BlockSpec(memory_space=pltpu.VMEM)],
        out_specs=pl.BlockSpec(memory_space=pltpu.VMEM),
        scratch_shapes=[
            pltpu.VMEM((TILE, TILE), jnp.float32),
            pltpu.VMEM((2, SUB, SUB, TILE), jnp.float32),
        ],
        cost_estimate=pl.CostEstimate(
            flops=200_000_000, bytes_accessed=4 * size * size * 2, transcendentals=size
        ),
        name="inverse_factor",
    )(gram)


def on_device(weights, momentum, gradient, warm_basis):
    rows, columns = momentum.shape
    owned = warm_basis.shape[0]
    depth = lax.axis_size("z")
    plane = lax.axis_size(PLANE)
    blocks = lax.axis_size(COLUMN_BLOCKS)
    rank = owned * depth * 2
    core = lax.axis_index("core")
    place = lax.axis_index("z")

    blended = momentum + gradient.astype(jnp.float32)
    partner = lax.ppermute(blended, "core", SWAP)
    basis = lax.all_gather(warm_basis, "z", axis=0, tiled=True)
    mine = dot(blended, basis, 1, 1)
    theirs = dot(partner, basis, 1, 1)
    partial = jnp.where(
        core == 0, jnp.stack([mine, theirs]), jnp.stack([theirs, mine])
    ).reshape(2 * rows, rank // 2)
    pieces = exchange(partial, PLANE).reshape(2, blocks, 2 * rows // plane, rank // 2)
    pieces = jnp.sum(pieces, axis=1)
    gathered = lax.broadcasted_iota(jnp.int32, (rank // 2, rank), 0)
    ranks = lax.broadcasted_iota(jnp.int32, (rank // 2, rank), 1)
    even = gathered // owned * (2 * owned) + gathered % owned
    part = dot(pieces[0], (ranks == even).astype(jnp.float32), 1, 0) + dot(
        pieces[1], (ranks == even + owned).astype(jnp.float32), 1, 0
    )
    projected = spread(part, PLANE, plane)

    half = lax.dynamic_slice_in_dim(projected, core * (rank // 2), rank // 2, 1)
    own_rows = lax.dynamic_slice_in_dim(half, core * rows, rows, 0)
    partner_rows = lax.dynamic_slice_in_dim(half, (1 - core) * rows, rows, 0)
    moved = dot(own_rows, blended, 0, 0) + dot(partner_rows, partner, 0, 0)
    tie = moved[0, 0] * 0.0
    moved = lax.psum_scatter(moved, "z", scatter_dimension=0, tiled=True)
    share = rank // plane
    mine_at = lax.axis_index(PLANE) * share
    gram_part = dot(lax.dynamic_slice_in_dim(projected, mine_at, share, 1), projected, 0, 0) + tie
    gram_row = jnp.sum(exchange(gram_part, "z").reshape(depth, share // depth, rank), axis=0)
    gram_share = spread(gram_row, "z", depth)
    gram = spread(gram_share, PLANE, plane)

    moved = lax.all_gather(moved, "z", axis=0, tiled=True)
    moved = spread(moved, "core", 2)

    inverse = inverse_factor(gram)
    own_projected = lax.dynamic_slice_in_dim(projected, core * rows, rows, 0)
    orthonormal = dot(own_projected, inverse, 1, 1)
    coefficients = dot(inverse, moved, 1, 0)
    energy = jnp.sum(coefficients * coefficients, axis=1).reshape(rank // 128, 128)
    energy = jnp.sum(
        spread(energy, COLUMN_BLOCKS, blocks).reshape(blocks, rank // 128, 128), axis=0
    ).reshape(rank)
    scale = lax.rsqrt(energy / FF + epsilon)
    feedback = dot(orthonormal, coefficients, 1, 0)
    new_momentum = blended - (1.0 - momentum_decay) * feedback
    update = dot(orthonormal * scale[None, :], coefficients, 1, 0)
    first = (place * 2 + core) * owned
    new_basis = (
        lax.dynamic_slice_in_dim(coefficients, first, owned, 0)
        * lax.dynamic_slice_in_dim(scale, first, owned, 0)[:, None]
    )
    new_weights = (weights.astype(jnp.float32) - step_size * math.sqrt(D / FF) * update).astype(
        jnp.bfloat16
    )
    return (new_weights, new_momentum, new_basis)


def solution(mesh):
    devices = mesh.devices
    split = Mesh(
        devices.reshape(devices.shape[0] // 2, 2, 4, devices.shape[1] // 4),
        ("z", "core", "x", "y"),
    )
    spec = P(("z", "core"), ("x", "y"))
    return jax.shard_map(
        on_device, mesh=split, in_specs=(spec,) * 4, out_specs=(spec,) * 3, check_vma=False
    )
```

```python
import math

import jax
import jax.numpy as jnp
from jax import lax
from jax.experimental import pallas as pl
from jax.experimental.pallas import tpu as pltpu
from jax.sharding import Mesh, PartitionSpec as P

D = 8192
FF = 14336

momentum_decay = 0.95
step_size = 2.0
epsilon = 1e-06

DEPTH = ("far", "near")
PLANE = ("x", "y", "core")
COLUMN_BLOCKS = ("x", "y")
HIGH = lax.Precision.HIGH
SWAP = [(0, 1), (1, 0)]


def dot(left_side, right_side, contract_left, contract_right, precision=lax.Precision.HIGHEST):
    return lax.dot_general(
        left_side,
        right_side,
        (((contract_left,), (contract_right,)), ((), ())),
        precision=precision,
        preferred_element_type=jnp.float32,
    )


def exchange(array, axes):
    return lax.all_to_all(array, axes, 0, 0, tiled=True)


def spread(array, axes, count):
    return exchange(
        jnp.broadcast_to(array[None], (count,) + array.shape).reshape(
            (count * array.shape[0],) + array.shape[1:]
        ),
        axes,
    )


SUB = 8
TILE = 128


def factor_step(work, wide, at):
    lane = lax.broadcasted_iota(jnp.int32,(SUB,TILE),1)
    sub = lax.broadcasted_iota(jnp.int32,(SUB,TILE),0)
    own = (lane>=at)&(lane<at+SUB)
    block = work[at:at+SUB,:]
    for j in range(SUB):
        wide[j] = jnp.broadcast_to(block[:,at+j:at+j+1],(SUB,TILE))
    work[at:at+SUB,:] = jnp.where(own, jnp.where(lane-at==sub,1.0,0.0), block)
    spread = lambda ref_row: jnp.broadcast_to(ref_row,(SUB,TILE))
    gram = [[spread(wide[j,i:i+1,:]) for j in range(i+1)] for i in range(SUB)]
    low = [[None]*SUB for _ in range(SUB)]
    inv = [None]*SUB
    rows = [None]*SUB
    for j in range(SUB):
        inv[j] = lax.rsqrt(gram[j][j])
        for i in range(j+1,SUB):
            low[i][j] = gram[i][j]*inv[j]
        for i in range(j+1,SUB):
            for m in range(j+1,i+1):
                gram[i][m] = gram[i][m]-low[i][j]*low[m][j]
        row = spread(work[at+j:at+j+1,:])
        for m in range(j):
            row = row - low[j][m]*rows[m]
        rows[j] = row*inv[j]
    out = rows[SUB-1]
    for i in range(SUB-1):
        out = jnp.where(sub==i, rows[i], out)
    work[at:at+SUB,:] = out
    nxt = at+SUB
    if nxt < TILE:
        block = work[nxt:nxt+SUB,:]
        left=[]
        total = jnp.where(own,0.0,block)
        for j in range(SUB):
            col = jnp.broadcast_to(block[:,at+j:at+j+1],(SUB,TILE))
            for m in range(j):
                col = col - left[m]*low[j][m]
            left.append(col*inv[j])
            total = total - left[j]*rows[j]
        work[nxt:nxt+SUB,:] = total
    far = nxt+SUB
    if far < TILE:
        prod = dot(out,out,0,0)
        rest = work[far:,:]
        lanes = lax.broadcasted_iota(jnp.int32,rest.shape,1)
        work[far:,:] = jnp.where((lanes>=at)&(lanes<at+SUB),0.0,rest) - prod[far:,:]


def inverse_factor_kernel(gram_ref, out_ref, work, wide):
    n = gram_ref.shape[0]; tiles = n//TILE
    out_ref[...] = gram_ref[...]
    def panel(p, carry):
        at = pl.multiple_of(p*TILE,TILE)
        work[...] = out_ref[pl.ds(at,TILE),pl.ds(at,TILE)]
        for k in range(TILE//SUB):
            factor_step(work, wide.at[k%2], k*SUB)
        r = lax.broadcasted_iota(jnp.int32,(TILE,TILE),0); c = lax.broadcasted_iota(jnp.int32,(TILE,TILE),1)
        inverse = jnp.where(r>=c, work[...], 0.0)
        out_ref[pl.ds(at,TILE),pl.ds(at,TILE)] = jnp.where(r==c,1.0,0.0)
        new = dot(inverse, out_ref[pl.ds(at,TILE),:],1,0)
        out_ref[pl.ds(at,TILE),:] = new
        for q in range(1,tiles):
            @pl.when(q>p)
            def _():
                out_ref[q*TILE:(q+1)*TILE,pl.ds(at,TILE)] = jnp.zeros((TILE,TILE),jnp.float32)
                out_ref[q*TILE:(q+1)*TILE,:] = out_ref[q*TILE:(q+1)*TILE,:] - dot(
                    new[:,q*TILE:(q+1)*TILE],new,0,0
                )
        return carry
    lax.fori_loop(0,tiles,panel,0)
    for q in range(tiles-1):
        out_ref[q*TILE:(q+1)*TILE,(q+1)*TILE:] = jnp.zeros((TILE,n-(q+1)*TILE),jnp.float32)


def inverse_factor(gram):
    size = gram.shape[0]
    return pl.pallas_call(
        inverse_factor_kernel,
        out_shape=jax.ShapeDtypeStruct((size, size), jnp.float32),
        in_specs=[pl.BlockSpec(memory_space=pltpu.VMEM)],
        out_specs=pl.BlockSpec(memory_space=pltpu.VMEM),
        scratch_shapes=[
            pltpu.VMEM((TILE, TILE), jnp.float32),
            pltpu.VMEM((2, SUB, SUB, TILE), jnp.float32),
        ],
        cost_estimate=pl.CostEstimate(
            flops=200_000_000, bytes_accessed=4 * size * size * 2, transcendentals=size
        ),
        compiler_params=pltpu.CompilerParams(vmem_limit_bytes=8 * 2**20),
        name="inverse_factor",
    )(gram)


def total(array, count):
    return jnp.sum(array.reshape((count, array.shape[0] // count) + array.shape[1:]), axis=0)


def by_core(core, own, other, axis):
    return jnp.where(
        core == 0, jnp.concatenate([own, other], axis), jnp.concatenate([other, own], axis)
    )


def on_device(weights, momentum, gradient, warm_basis):
    rows, columns = momentum.shape
    owned = warm_basis.shape[0]
    depth = lax.axis_size(DEPTH)
    plane = lax.axis_size(PLANE)
    blocks = lax.axis_size(COLUMN_BLOCKS)
    far, near = lax.axis_size("far"), lax.axis_size("near")
    rank = owned * depth * 2
    half = rank // 2
    core = lax.axis_index("core")
    place = lax.axis_index(DEPTH)

    blended = momentum + gradient.astype(jnp.float32)
    partner = lax.ppermute(blended, "core", SWAP)
    basis = lax.all_gather(warm_basis, DEPTH, axis=0, tiled=True)
    partial = jnp.concatenate([dot(blended, basis, 1, 1), dot(partner, basis, 1, 1)])
    part = total(exchange(partial, COLUMN_BLOCKS), blocks)
    projected = spread(part, COLUMN_BLOCKS, blocks)
    others = lax.ppermute(projected, "core", SWAP)
    others = jnp.concatenate([others[rows:], others[:rows]])

    def natural(first, count):
        kept = lax.broadcasted_iota(jnp.int32, (rank, count), 0)
        ranks = lax.broadcasted_iota(jnp.int32, (rank, count), 1) + first
        source = ranks // owned % 2 * half + ranks // (2 * owned) * owned + ranks % owned
        return (kept == source).astype(jnp.float32)

    order = natural(0, rank)
    joined = by_core(core, projected, others, 1)
    mine = dot(joined, natural(core * half, half), 1, 0)
    moved = dot(mine[:rows], blended, 0, 0, HIGH) + dot(mine[rows:], partner, 0, 0, HIGH)
    moved = lax.psum_scatter(moved, DEPTH, scatter_dimension=0, tiled=True)

    share = half // blocks
    picked = lax.dynamic_slice_in_dim(
        projected, lax.axis_index(COLUMN_BLOCKS) * share, share, 1
    )
    same = dot(picked, projected, 0, 0)
    cross = dot(picked, others, 0, 0)
    gram = dot(by_core(core, same, cross, 1), order, 1, 0)
    gram = total(spread(gram, "far", far), far)
    gram = total(spread(gram, "near", near), near)
    gram = spread(gram, PLANE, plane)
    inverse = inverse_factor(gram)

    moved = lax.all_gather(moved, DEPTH, axis=0, tiled=True)
    moved = spread(moved, "core", 2)
    own_projected = dot(joined[:rows], order, 1, 0)
    orthonormal = dot(own_projected, inverse, 1, 1, HIGH)
    coefficients = dot(inverse, moved, 1, 0, HIGH)
    energy = jnp.sum(coefficients * coefficients, axis=1).reshape(rank // 128, 128)
    energy = total(spread(energy, COLUMN_BLOCKS, blocks), blocks).reshape(rank)
    scale = lax.rsqrt(energy / FF + epsilon)
    feedback = dot(orthonormal, coefficients, 1, 0, HIGH)
    new_momentum = blended - (1.0 - momentum_decay) * feedback
    update = dot(orthonormal * scale[None, :], coefficients, 1, 0, HIGH)
    first = (place * 2 + core) * owned
    new_basis = (
        lax.dynamic_slice_in_dim(coefficients, first, owned, 0)
        * lax.dynamic_slice_in_dim(scale, first, owned, 0)[:, None]
    )
    new_weights = (weights.astype(jnp.float32) - step_size * math.sqrt(D / FF) * update).astype(
        jnp.bfloat16
    )
    return (new_weights, new_momentum, new_basis)


def solution(mesh):
    devices = mesh.devices
    split = Mesh(
        devices.reshape(4, devices.shape[0] // 8, 2, 4, devices.shape[1] // 4),
        ("far", "near", "core", "x", "y"),
    )
    spec = P(("far", "near", "core"), ("x", "y"))
    return jax.shard_map(
        on_device, mesh=split, in_specs=(spec,) * 4, out_specs=(spec,) * 3, check_vma=False
    )
```

```python
import functools
import math

import jax
import jax.numpy as jnp
from jax import lax
from jax.experimental import pallas as pl
from jax.experimental.pallas import tpu as pltpu
from jax.sharding import Mesh, PartitionSpec as P

D = 8192
FF = 14336

momentum_decay = 0.95
step_size = 2.0
epsilon = 1e-06

DEPTH = ("far", "near")
COLUMN_BLOCKS = ("x", "y")
HIGH = lax.Precision.HIGH
SWAP = [(0, 1), (1, 0)]


def dot(left_side, right_side, contract_left, contract_right, precision=lax.Precision.HIGHEST):
    return lax.dot_general(
        left_side,
        right_side,
        (((contract_left,), (contract_right,)), ((), ())),
        precision=precision,
        preferred_element_type=jnp.float32,
    )


def exchange(array, axes):
    return lax.all_to_all(array, axes, 0, 0, tiled=True)


def spread(array, axes, count):
    return exchange(
        jnp.broadcast_to(array[None], (count,) + array.shape).reshape(
            (count * array.shape[0],) + array.shape[1:]
        ),
        axes,
    )


SUB = 8
TILE = 128


def factor_step(work, wide, at, block):
    lane = lax.broadcasted_iota(jnp.int32,(SUB,TILE),1)
    sub = lax.broadcasted_iota(jnp.int32,(SUB,TILE),0)
    own = (lane>=at)&(lane<at+SUB)
    for j in range(SUB):
        wide[j] = jnp.broadcast_to(block[:,at+j:at+j+1],(SUB,TILE))
    work[at:at+SUB,:] = jnp.where(own, jnp.where(lane-at==sub,1.0,0.0), block)
    spread = lambda ref_row: jnp.broadcast_to(ref_row,(SUB,TILE))
    gram = [[spread(wide[j,i:i+1,:]) for j in range(i+1)] for i in range(SUB)]
    low = [[None]*SUB for _ in range(SUB)]
    inv = [None]*SUB
    rows = [None]*SUB
    for j in range(SUB):
        inv[j] = lax.rsqrt(gram[j][j])
        for i in range(j+1,SUB):
            low[i][j] = gram[i][j]*inv[j]
        for i in range(j+1,SUB):
            for m in range(j+1,i+1):
                gram[i][m] = gram[i][m]-low[i][j]*low[m][j]
        row = spread(work[at+j:at+j+1,:])
        for m in range(j):
            row = row - low[j][m]*rows[m]
        rows[j] = row*inv[j]
    out = rows[SUB-1]
    for i in range(SUB-1):
        out = jnp.where(sub==i, rows[i], out)
    work[at:at+SUB,:] = out
    far = at+SUB*4
    ahead = None
    for nxt in range(at+SUB, min(far,TILE), SUB):
        block = work[nxt:nxt+SUB,:]
        left=[]
        total = jnp.where(own,0.0,block)
        for j in range(SUB):
            col = jnp.broadcast_to(block[:,at+j:at+j+1],(SUB,TILE))
            for m in range(j):
                col = col - left[m]*low[j][m]
            left.append(col*inv[j])
            total = total - left[j]*rows[j]
        if nxt == at+SUB:
            ahead = total
        else:
            work[nxt:nxt+SUB,:] = total
    if far < TILE:
        prod = dot(out,out,0,0)
        rest = work[far:,:]
        lanes = lax.broadcasted_iota(jnp.int32,rest.shape,1)
        work[far:,:] = jnp.where((lanes>=at)&(lanes<at+SUB),0.0,rest) - prod[far:,:]
    return ahead


def inverse_factor_kernel(core_ref, own_ref, other_ref, out_ref, work, wide, *, owned):
    n = out_ref.shape[0]
    tiles = n//TILE
    core = core_ref[0]
    for t in range(n // (2 * owned)):
        first = pl.multiple_of(2 * t * owned + core * owned, owned)
        second = pl.multiple_of(2 * t * owned + (1 - core) * owned, owned)
        out_ref[pl.ds(first, owned), :] = own_ref[t*owned:(t+1)*owned, :]
        out_ref[pl.ds(second, owned), :] = other_ref[t*owned:(t+1)*owned, :]
    def panel(p, carry):
        at = pl.multiple_of(p*TILE,TILE)
        work[...] = out_ref[pl.ds(at,TILE),pl.ds(at,TILE)]
        block = work[0:SUB,:]
        for k in range(TILE//SUB):
            block = factor_step(work, wide.at[k%2], k*SUB, block)
        r = lax.broadcasted_iota(jnp.int32,(TILE,TILE),0); c = lax.broadcasted_iota(jnp.int32,(TILE,TILE),1)
        inverse = jnp.where(r>=c, work[...], 0.0)
        out_ref[pl.ds(at,TILE),pl.ds(at,TILE)] = jnp.where(r==c,1.0,0.0)
        new = dot(inverse, out_ref[pl.ds(at,TILE),:],1,0)
        out_ref[pl.ds(at,TILE),:] = new
        for q in range(1,tiles):
            @pl.when(q>p)
            def _():
                out_ref[q*TILE:(q+1)*TILE,pl.ds(at,TILE)] = jnp.zeros((TILE,TILE),jnp.float32)
                out_ref[q*TILE:(q+1)*TILE,:] = out_ref[q*TILE:(q+1)*TILE,:] - dot(new[:,q*TILE:(q+1)*TILE],new,0,0)
        return carry
    lax.fori_loop(0,tiles,panel,0)
    for q in range(tiles-1):
        out_ref[q*TILE:(q+1)*TILE,(q+1)*TILE:] = jnp.zeros((TILE,n-(q+1)*TILE),jnp.float32)

def inverse_factor(core, own, other, owned):
    size = own.shape[1]
    whole = pl.BlockSpec(memory_space=pltpu.VMEM)
    return pl.pallas_call(
        functools.partial(inverse_factor_kernel, owned=owned),
        out_shape=jax.ShapeDtypeStruct((size, size), jnp.float32),
        in_specs=[pl.BlockSpec(memory_space=pltpu.SMEM), whole, whole],
        out_specs=whole,
        scratch_shapes=[
            pltpu.VMEM((TILE, TILE), jnp.float32),
            pltpu.VMEM((2, SUB, SUB, TILE), jnp.float32),
        ],
        cost_estimate=pl.CostEstimate(
            flops=200_000_000, bytes_accessed=4 * size * size * 2, transcendentals=size
        ),
        compiler_params=pltpu.CompilerParams(vmem_limit_bytes=8 * 2**20),
        name="inverse_factor",
    )(core.reshape(1), own, other)


def total(array, count):
    return jnp.sum(array.reshape((count, array.shape[0] // count) + array.shape[1:]), axis=0)


def by_core(core, own, other, axis):
    return jnp.where(
        core == 0, jnp.concatenate([own, other], axis), jnp.concatenate([other, own], axis)
    )


def one_side(rank, owned, core):
    ranks = lax.broadcasted_iota(jnp.int32, (rank, rank // 2), 0)
    kept = lax.broadcasted_iota(jnp.int32, (rank, rank // 2), 1)
    source = (kept // owned * 2 + core) * owned + kept % owned
    return (ranks == source).astype(jnp.float32)


def on_device(weights, momentum, gradient, warm_basis):
    rows, columns = momentum.shape
    owned = warm_basis.shape[0]
    depth = lax.axis_size(DEPTH)
    blocks = lax.axis_size(COLUMN_BLOCKS)
    far, near = lax.axis_size("far"), lax.axis_size("near")
    rank = owned * depth * 2
    half = rank // 2
    core = lax.axis_index("core")
    place = lax.axis_index(DEPTH)

    blended = momentum + gradient.astype(jnp.float32)
    partner = lax.ppermute(blended, "core", SWAP)
    basis = lax.all_gather(warm_basis, DEPTH, axis=0, tiled=True)
    partial = jnp.concatenate([dot(blended, basis, 1, 1), dot(partner, basis, 1, 1)])
    part = total(exchange(partial, COLUMN_BLOCKS), blocks)
    projected = spread(part, COLUMN_BLOCKS, blocks)
    others = lax.ppermute(projected, "core", SWAP)
    others = jnp.concatenate([others[rows:], others[:rows]])

    moved = dot(projected[:rows], blended, 0, 0, HIGH) + dot(
        projected[rows:], partner, 0, 0, HIGH
    )
    moved = lax.psum_scatter(moved, DEPTH, scatter_dimension=0, tiled=True)

    kept = lax.broadcasted_iota(jnp.int32, (rank, rank), 0)
    ranks = lax.broadcasted_iota(jnp.int32, (rank, rank), 1)
    source = ranks // owned % 2 * half + ranks // (2 * owned) * owned + ranks % owned
    order = (kept == source).astype(jnp.float32)

    share = half // blocks
    picked = lax.dynamic_slice_in_dim(
        projected, lax.axis_index(COLUMN_BLOCKS) * share, share, 1
    )
    same = dot(picked, projected, 0, 0)
    cross = dot(picked, others, 0, 0)
    gram = dot(by_core(core, same, cross, 1), order, 1, 0)
    gram = total(spread(gram, "far", far), far)
    gram = total(spread(gram, "near", near), near)
    gram = spread(gram, COLUMN_BLOCKS, blocks)
    inverse = inverse_factor(core, gram, lax.ppermute(gram, "core", SWAP), owned)

    moved = lax.all_gather(moved + inverse[0, rank - 1], DEPTH, axis=0, tiled=True)
    handed = lax.ppermute(moved, "core", SWAP)
    joined = by_core(core, projected[:rows], others[:rows], 1)
    own_projected = dot(joined, order, 1, 0)
    orthonormal = dot(own_projected, inverse, 1, 1, HIGH)
    coefficients = dot(
        dot(inverse, one_side(rank, owned, core), 1, 0, HIGH), moved, 1, 0, HIGH
    ) + dot(dot(inverse, one_side(rank, owned, 1 - core), 1, 0, HIGH), handed, 1, 0, HIGH)
    energy = jnp.sum(coefficients * coefficients, axis=1).reshape(rank // 128, 128)
    energy = total(spread(energy, COLUMN_BLOCKS, blocks), blocks).reshape(rank)
    scale = lax.rsqrt(energy / FF + epsilon)
    feedback = dot(orthonormal, coefficients, 1, 0, HIGH)
    new_momentum = blended - (1.0 - momentum_decay) * feedback
    update = dot(orthonormal * scale[None, :], coefficients, 1, 0, HIGH)
    first = (place * 2 + core) * owned
    new_basis = (
        lax.dynamic_slice_in_dim(coefficients, first, owned, 0)
        * lax.dynamic_slice_in_dim(scale, first, owned, 0)[:, None]
    )
    new_weights = (weights.astype(jnp.float32) - step_size * math.sqrt(D / FF) * update).astype(
        jnp.bfloat16
    )
    return (new_weights, new_momentum, new_basis)


def solution(mesh):
    devices = mesh.devices
    split = Mesh(
        devices.reshape(4, devices.shape[0] // 8, 2, 4, devices.shape[1] // 4),
        ("far", "near", "core", "x", "y"),
    )
    spec = P(("far", "near", "core"), ("x", "y"))
    return jax.shard_map(
        on_device, mesh=split, in_specs=(spec,) * 4, out_specs=(spec,) * 3, check_vma=False
    )
```

```python
import functools
import math

import jax
import jax.numpy as jnp
from jax import lax
from jax.experimental import pallas as pl
from jax.experimental.pallas import tpu as pltpu
from jax.sharding import Mesh, PartitionSpec as P

D = 8192
FF = 14336

momentum_decay = 0.95
step_size = 2.0
epsilon = 1e-06

DEPTH = ("far", "near")
COLUMN_BLOCKS = ("x", "y")
HIGH = lax.Precision.HIGH
SWAP = [(0, 1), (1, 0)]


def dot(left_side, right_side, contract_left, contract_right, precision=lax.Precision.HIGHEST):
    return lax.dot_general(
        left_side,
        right_side,
        (((contract_left,), (contract_right,)), ((), ())),
        precision=precision,
        preferred_element_type=jnp.float32,
    )


def exchange(array, axes):
    return lax.all_to_all(array, axes, 0, 0, tiled=True)


def spread(array, axes, count):
    return exchange(
        jnp.broadcast_to(array[None], (count,) + array.shape).reshape(
            (count * array.shape[0],) + array.shape[1:]
        ),
        axes,
    )


SUB = 8
TILE = 128


def factor_step(work, wide, at, block):
    lane = lax.broadcasted_iota(jnp.int32,(SUB,TILE),1)
    sub = lax.broadcasted_iota(jnp.int32,(SUB,TILE),0)
    own = (lane>=at)&(lane<at+SUB)
    for j in range(SUB):
        wide[j] = jnp.broadcast_to(block[:,at+j:at+j+1],(SUB,TILE))
    work[at:at+SUB,:] = jnp.where(own, jnp.where(lane-at==sub,1.0,0.0), block)
    spread = lambda ref_row: jnp.broadcast_to(ref_row,(SUB,TILE))
    gram = [[spread(wide[j,i:i+1,:]) for j in range(i+1)] for i in range(SUB)]
    low = [[None]*SUB for _ in range(SUB)]
    inv = [None]*SUB
    rows = [None]*SUB
    for j in range(SUB):
        inv[j] = lax.rsqrt(gram[j][j])
        for i in range(j+1,SUB):
            low[i][j] = gram[i][j]*inv[j]
        for i in range(j+1,SUB):
            for m in range(j+1,i+1):
                gram[i][m] = gram[i][m]-low[i][j]*low[m][j]
        row = spread(work[at+j:at+j+1,:])
        for m in range(j):
            row = row - low[j][m]*rows[m]
        rows[j] = row*inv[j]
    out = rows[SUB-1]
    for i in range(SUB-1):
        out = jnp.where(sub==i, rows[i], out)
    work[at:at+SUB,:] = out
    far = at+SUB*4
    ahead = None
    for nxt in range(at+SUB, min(far,TILE), SUB):
        block = work[nxt:nxt+SUB,:]
        left=[]
        total = jnp.where(own,0.0,block)
        for j in range(SUB):
            col = jnp.broadcast_to(block[:,at+j:at+j+1],(SUB,TILE))
            for m in range(j):
                col = col - left[m]*low[j][m]
            left.append(col*inv[j])
            total = total - left[j]*rows[j]
        if nxt == at+SUB:
            ahead = total
        else:
            work[nxt:nxt+SUB,:] = total
    if far < TILE:
        prod = dot(out,out,0,0)
        rest = work[far:,:]
        lanes = lax.broadcasted_iota(jnp.int32,rest.shape,1)
        work[far:,:] = jnp.where((lanes>=at)&(lanes<at+SUB),0.0,rest) - prod[far:,:]
    return ahead


def inverse_factor_kernel(core_ref, own_ref, other_ref, out_ref, work, wide, *, owned):
    n = out_ref.shape[0]
    tiles = n//TILE
    core = core_ref[0]
    for t in range(n // (2 * owned)):
        first = pl.multiple_of(2 * t * owned + core * owned, owned)
        second = pl.multiple_of(2 * t * owned + (1 - core) * owned, owned)
        out_ref[pl.ds(first, owned), :] = own_ref[t*owned:(t+1)*owned, :]
        out_ref[pl.ds(second, owned), :] = other_ref[t*owned:(t+1)*owned, :]
    def panel(p, carry):
        at = pl.multiple_of(p*TILE,TILE)
        work[...] = out_ref[pl.ds(at,TILE),pl.ds(at,TILE)]
        block = work[0:SUB,:]
        for k in range(TILE//SUB):
            block = factor_step(work, wide.at[k%2], k*SUB, block)
        r = lax.broadcasted_iota(jnp.int32,(TILE,TILE),0); c = lax.broadcasted_iota(jnp.int32,(TILE,TILE),1)
        inverse = jnp.where(r>=c, work[...], 0.0)
        out_ref[pl.ds(at,TILE),pl.ds(at,TILE)] = jnp.where(r==c,1.0,0.0)
        new = dot(inverse, out_ref[pl.ds(at,TILE),:],1,0)
        out_ref[pl.ds(at,TILE),:] = new
        for q in range(1,tiles):
            @pl.when(q>p)
            def _():
                out_ref[q*TILE:(q+1)*TILE,pl.ds(at,TILE)] = jnp.zeros((TILE,TILE),jnp.float32)
                out_ref[q*TILE:(q+1)*TILE,:] = out_ref[q*TILE:(q+1)*TILE,:] - dot(new[:,q*TILE:(q+1)*TILE],new,0,0)
        return carry
    lax.fori_loop(0,tiles,panel,0)
    for q in range(tiles-1):
        out_ref[q*TILE:(q+1)*TILE,(q+1)*TILE:] = jnp.zeros((TILE,n-(q+1)*TILE),jnp.float32)

def inverse_factor(core, own, other, owned):
    size = own.shape[1]
    whole = pl.BlockSpec(memory_space=pltpu.VMEM)
    return pl.pallas_call(
        functools.partial(inverse_factor_kernel, owned=owned),
        out_shape=jax.ShapeDtypeStruct((size, size), jnp.float32),
        in_specs=[pl.BlockSpec(memory_space=pltpu.SMEM), whole, whole],
        out_specs=whole,
        scratch_shapes=[
            pltpu.VMEM((TILE, TILE), jnp.float32),
            pltpu.VMEM((2, SUB, SUB, TILE), jnp.float32),
        ],
        cost_estimate=pl.CostEstimate(
            flops=8_000_000_000, bytes_accessed=4 * size * size * 2, transcendentals=size
        ),
        compiler_params=pltpu.CompilerParams(vmem_limit_bytes=8 * 2**20),
        name="inverse_factor",
    )(core.reshape(1), own, other)


def total(array, count):
    return jnp.sum(array.reshape((count, array.shape[0] // count) + array.shape[1:]), axis=0)


def by_core(core, own, other, axis):
    return jnp.where(
        core == 0, jnp.concatenate([own, other], axis), jnp.concatenate([other, own], axis)
    )


def one_side(rank, owned, core):
    ranks = lax.broadcasted_iota(jnp.int32, (rank, rank // 2), 0)
    kept = lax.broadcasted_iota(jnp.int32, (rank, rank // 2), 1)
    source = (kept // owned * 2 + core) * owned + kept % owned
    return (ranks == source).astype(jnp.float32)


def on_device(weights, momentum, gradient, warm_basis):
    rows, columns = momentum.shape
    owned = warm_basis.shape[0]
    depth = lax.axis_size(DEPTH)
    blocks = lax.axis_size(COLUMN_BLOCKS)
    rank = owned * depth * 2
    half = rank // 2
    core = lax.axis_index("core")
    place = lax.axis_index(DEPTH)

    blended = momentum + gradient.astype(jnp.float32)
    partner = lax.ppermute(blended, "core", SWAP)
    basis = lax.all_gather(warm_basis, DEPTH, axis=0, tiled=True)
    partial = jnp.concatenate([dot(blended, basis, 1, 1), dot(partner, basis, 1, 1)])
    part = total(exchange(partial, COLUMN_BLOCKS), blocks)
    projected = spread(part, COLUMN_BLOCKS, blocks)
    others = lax.ppermute(projected, "core", SWAP)
    others = jnp.concatenate([others[rows:], others[:rows]])

    moved = dot(projected[:rows], blended, 0, 0, HIGH) + dot(
        projected[rows:], partner, 0, 0, HIGH
    )
    moved = total(exchange(moved, DEPTH), depth)

    kept = lax.broadcasted_iota(jnp.int32, (rank, rank), 0)
    ranks = lax.broadcasted_iota(jnp.int32, (rank, rank), 1)
    source = ranks // owned % 2 * half + ranks // (2 * owned) * owned + ranks % owned
    order = (kept == source).astype(jnp.float32)

    share = half // blocks
    picked = lax.dynamic_slice_in_dim(
        projected, lax.axis_index(COLUMN_BLOCKS) * share, share, 1
    )
    same = dot(picked, projected, 0, 0)
    cross = dot(picked, others, 0, 0)
    gram = dot(by_core(core, same, cross, 1), order, 1, 0)
    gram = total(lax.all_gather(gram, DEPTH, axis=0, tiled=True), depth)
    gram = spread(gram + moved[0, 0] * 0.0, COLUMN_BLOCKS, blocks)
    moved = spread(moved + gram[0, 0] * 0.0, DEPTH, depth)
    inverse = inverse_factor(core, gram, lax.ppermute(gram, "core", SWAP), owned)
    handed = lax.ppermute(moved, "core", SWAP)
    joined = by_core(core, projected[:rows], others[:rows], 1)
    own_projected = dot(joined, order, 1, 0)
    orthonormal = dot(own_projected, inverse, 1, 1, HIGH)
    coefficients = dot(
        dot(inverse, one_side(rank, owned, core), 1, 0, HIGH), moved, 1, 0, HIGH
    ) + dot(dot(inverse, one_side(rank, owned, 1 - core), 1, 0, HIGH), handed, 1, 0, HIGH)
    energy = jnp.sum(coefficients * coefficients, axis=1).reshape(rank // 128, 128)
    energy = total(spread(energy, COLUMN_BLOCKS, blocks), blocks).reshape(rank)
    scale = lax.rsqrt(energy / FF + epsilon)
    feedback = dot(orthonormal, coefficients, 1, 0, HIGH)
    new_momentum = blended - (1.0 - momentum_decay) * feedback
    update = dot(orthonormal * scale[None, :], coefficients, 1, 0, HIGH)
    first = (place * 2 + core) * owned
    new_basis = (
        lax.dynamic_slice_in_dim(coefficients, first, owned, 0)
        * lax.dynamic_slice_in_dim(scale, first, owned, 0)[:, None]
    )
    new_weights = (weights.astype(jnp.float32) - step_size * math.sqrt(D / FF) * update).astype(
        jnp.bfloat16
    )
    return (new_weights, new_momentum, new_basis)


def solution(mesh):
    devices = mesh.devices
    split = Mesh(
        devices.reshape(4, devices.shape[0] // 8, 2, 4, devices.shape[1] // 4),
        ("far", "near", "core", "x", "y"),
    )
    spec = P(("far", "near", "core"), ("x", "y"))
    return jax.shard_map(
        on_device, mesh=split, in_specs=(spec,) * 4, out_specs=(spec,) * 3, check_vma=False
    )
```

```python
import functools
import math

import jax
import jax.numpy as jnp
from jax import lax
from jax.experimental import pallas as pl
from jax.experimental.pallas import tpu as pltpu
from jax.sharding import Mesh, PartitionSpec as P

D = 8192
FF = 14336

momentum_decay = 0.95
step_size = 2.0
epsilon = 1e-06

DEPTH = ("far", "near")
COLUMN_BLOCKS = ("x", "y")
HIGH = lax.Precision.HIGH
SWAP = [(0, 1), (1, 0)]


def dot(left_side, right_side, contract_left, contract_right, precision=lax.Precision.HIGHEST):
    return lax.dot_general(
        left_side,
        right_side,
        (((contract_left,), (contract_right,)), ((), ())),
        precision=precision,
        preferred_element_type=jnp.float32,
    )


def exchange(array, axes):
    return lax.all_to_all(array, axes, 0, 0, tiled=True)


def spread(array, axes, count):
    return exchange(
        jnp.broadcast_to(array[None], (count,) + array.shape).reshape(
            (count * array.shape[0],) + array.shape[1:]
        ),
        axes,
    )


SUB = 8
TILE = 128
GROUP = 32


def factor_step(work, wide, at, block):
    lane = lax.broadcasted_iota(jnp.int32,(SUB,TILE),1)
    sub = lax.broadcasted_iota(jnp.int32,(SUB,TILE),0)
    own = (lane>=at)&(lane<at+SUB)
    for j in range(SUB):
        wide[j] = jnp.broadcast_to(block[:,at+j:at+j+1],(SUB,TILE))
    work[at:at+SUB,:] = jnp.where(own, jnp.where(lane-at==sub,1.0,0.0), block)
    spread = lambda ref_row: jnp.broadcast_to(ref_row,(SUB,TILE))
    gram = [[spread(wide[j,i:i+1,:]) for j in range(i+1)] for i in range(SUB)]
    low = [[None]*SUB for _ in range(SUB)]
    inv = [None]*SUB
    rows = [None]*SUB
    for j in range(SUB):
        inv[j] = lax.rsqrt(gram[j][j])
        for i in range(j+1,SUB):
            low[i][j] = gram[i][j]*inv[j]
        for i in range(j+1,SUB):
            for m in range(j+1,i+1):
                gram[i][m] = gram[i][m]-low[i][j]*low[m][j]
        row = spread(work[at+j:at+j+1,:])
        for m in range(j):
            row = row - low[j][m]*rows[m]
        rows[j] = row*inv[j]
    out = rows[SUB-1]
    for i in range(SUB-1):
        out = jnp.where(sub==i, rows[i], out)
    work[at:at+SUB,:] = out
    far = (at//GROUP+2)*GROUP
    ahead = None
    for nxt in range(at+SUB, min(far,TILE), SUB):
        block = work[nxt:nxt+SUB,:]
        left=[]
        total = jnp.where(own,0.0,block)
        for j in range(SUB):
            col = jnp.broadcast_to(block[:,at+j:at+j+1],(SUB,TILE))
            for m in range(j):
                col = col - left[m]*low[j][m]
            left.append(col*inv[j])
            total = total - left[j]*rows[j]
        if nxt == at+SUB:
            ahead = total
        else:
            work[nxt:nxt+SUB,:] = total
    return ahead


def group_step(work, at):
    far = at+2*GROUP
    if far < TILE:
        rows = work[at:at+GROUP,:]
        lane = lax.broadcasted_iota(jnp.int32,(GROUP,TILE),1)-at
        sub = lax.broadcasted_iota(jnp.int32,(GROUP,TILE),0)
        clean = jnp.where((lane>=sub//SUB*SUB+SUB)&(lane<GROUP),0.0,rows)
        prod = dot(rows,clean,0,0)
        rest = work[far:,:]
        lanes = lax.broadcasted_iota(jnp.int32,rest.shape,1)
        work[far:,:] = jnp.where((lanes>=at)&(lanes<at+GROUP),0.0,rest) - prod[far:,:]


def inverse_factor_kernel(
    core_ref, own_ref, other_ref, out_ref, zero_ref, work, wide, *, owned
):
    n = out_ref.shape[0]
    tiles = n//TILE
    core = core_ref[0]
    for t in range(n // (2 * owned)):
        first = pl.multiple_of(2 * t * owned + core * owned, owned)
        second = pl.multiple_of(2 * t * owned + (1 - core) * owned, owned)
        out_ref[pl.ds(first, owned), :] = own_ref[t*owned:(t+1)*owned, :]
        out_ref[pl.ds(second, owned), :] = other_ref[t*owned:(t+1)*owned, :]
    def panel(p, carry):
        at = pl.multiple_of(p*TILE,TILE)
        work[...] = out_ref[pl.ds(at,TILE),pl.ds(at,TILE)]
        block = work[0:SUB,:]
        for k in range(TILE//SUB):
            block = factor_step(work, wide.at[k%2], k*SUB, block)
            if (k+1)*SUB%GROUP==0:
                group_step(work,(k+1)*SUB-GROUP)
        r = lax.broadcasted_iota(jnp.int32,(TILE,TILE),0); c = lax.broadcasted_iota(jnp.int32,(TILE,TILE),1)
        inverse = jnp.where(r>=c, work[...], 0.0)
        out_ref[pl.ds(at,TILE),pl.ds(at,TILE)] = jnp.where(r==c,1.0,0.0)
        new = dot(inverse, out_ref[pl.ds(at,TILE),:],1,0)
        out_ref[pl.ds(at,TILE),:] = new
        for q in range(1,tiles):
            @pl.when(q>p)
            def _():
                out_ref[q*TILE:(q+1)*TILE,pl.ds(at,TILE)] = jnp.zeros((TILE,TILE),jnp.float32)
                out_ref[q*TILE:(q+1)*TILE,:] = out_ref[q*TILE:(q+1)*TILE,:] - dot(new[:,q*TILE:(q+1)*TILE],new,0,0)
        return carry
    lax.fori_loop(0,tiles,panel,0)
    for q in range(tiles-1):
        out_ref[q*TILE:(q+1)*TILE,(q+1)*TILE:] = jnp.zeros((TILE,n-(q+1)*TILE),jnp.float32)
    zero_ref[...] = jnp.zeros_like(zero_ref)

def inverse_factor(core, own, other, owned, columns):
    size = own.shape[1]
    whole = pl.BlockSpec(memory_space=pltpu.VMEM)
    return pl.pallas_call(
        functools.partial(inverse_factor_kernel, owned=owned),
        out_shape=(
            jax.ShapeDtypeStruct((size, size), jnp.float32),
            jax.ShapeDtypeStruct((owned, columns), jnp.float32),
        ),
        in_specs=[pl.BlockSpec(memory_space=pltpu.SMEM), whole, whole],
        out_specs=(whole, whole),
        scratch_shapes=[
            pltpu.VMEM((TILE, TILE), jnp.float32),
            pltpu.VMEM((2, SUB, SUB, TILE), jnp.float32),
        ],
        cost_estimate=pl.CostEstimate(
            flops=200_000_000, bytes_accessed=4 * size * size * 2, transcendentals=size
        ),
        compiler_params=pltpu.CompilerParams(vmem_limit_bytes=8 * 2**20),
        name="inverse_factor",
    )(core.reshape(1), own, other)


def total(array, count):
    return jnp.sum(array.reshape((count, array.shape[0] // count) + array.shape[1:]), axis=0)


def by_core(core, own, other, axis):
    return jnp.where(
        core == 0, jnp.concatenate([own, other], axis), jnp.concatenate([other, own], axis)
    )


def one_side(rank, owned, core):
    ranks = lax.broadcasted_iota(jnp.int32, (rank, rank // 2), 0)
    kept = lax.broadcasted_iota(jnp.int32, (rank, rank // 2), 1)
    source = (kept // owned * 2 + core) * owned + kept % owned
    return (ranks == source).astype(jnp.float32)


def on_device(weights, momentum, gradient, warm_basis):
    rows, columns = momentum.shape
    owned = warm_basis.shape[0]
    depth = lax.axis_size(DEPTH)
    blocks = lax.axis_size(COLUMN_BLOCKS)
    far, near = lax.axis_size("far"), lax.axis_size("near")
    rank = owned * depth * 2
    half = rank // 2
    core = lax.axis_index("core")
    place = lax.axis_index(DEPTH)

    blended = momentum + gradient.astype(jnp.float32)
    partner = lax.ppermute(blended, "core", SWAP)
    basis = lax.all_gather(warm_basis, DEPTH, axis=0, tiled=True)
    partial = jnp.concatenate([dot(blended, basis, 1, 1), dot(partner, basis, 1, 1)])
    part = total(exchange(partial, COLUMN_BLOCKS), blocks)
    projected = spread(part, COLUMN_BLOCKS, blocks)
    others = lax.ppermute(projected, "core", SWAP)
    others = jnp.concatenate([others[rows:], others[:rows]])

    moved = dot(projected[:rows], blended, 0, 0, HIGH) + dot(
        projected[rows:], partner, 0, 0, HIGH
    )
    moved = lax.psum_scatter(moved, DEPTH, scatter_dimension=0, tiled=True)

    kept = lax.broadcasted_iota(jnp.int32, (rank, rank), 0)
    ranks = lax.broadcasted_iota(jnp.int32, (rank, rank), 1)
    source = ranks // owned % 2 * half + ranks // (2 * owned) * owned + ranks % owned
    order = (kept == source).astype(jnp.float32)

    share = half // blocks
    picked = lax.dynamic_slice_in_dim(
        projected, lax.axis_index(COLUMN_BLOCKS) * share, share, 1
    )
    same = dot(picked, projected, 0, 0)
    cross = dot(picked, others, 0, 0)
    gram = dot(by_core(core, same, cross, 1), order, 1, 0)
    gram = total(spread(gram, "far", far), far)
    gram = total(spread(gram, "near", near), near)
    gram = spread(gram, COLUMN_BLOCKS, blocks)
    inverse, zero = inverse_factor(
        core, gram, lax.ppermute(gram, "core", SWAP), owned, columns
    )

    moved = lax.all_gather(moved + zero, DEPTH, axis=0, tiled=True)
    handed = lax.ppermute(moved, "core", SWAP)
    joined = by_core(core, projected[:rows], others[:rows], 1)
    own_projected = dot(joined, order, 1, 0)
    orthonormal = dot(own_projected, inverse, 1, 1, HIGH)
    coefficients = dot(
        dot(inverse, one_side(rank, owned, core), 1, 0, HIGH), moved, 1, 0, HIGH
    ) + dot(dot(inverse, one_side(rank, owned, 1 - core), 1, 0, HIGH), handed, 1, 0, HIGH)
    energy = jnp.sum(coefficients * coefficients, axis=1).reshape(rank // 128, 128)
    energy = total(spread(energy, COLUMN_BLOCKS, blocks), blocks).reshape(rank)
    scale = lax.rsqrt(energy / FF + epsilon)
    feedback = dot(orthonormal, coefficients, 1, 0, HIGH)
    new_momentum = blended - (1.0 - momentum_decay) * feedback
    update = dot(orthonormal * scale[None, :], coefficients, 1, 0, HIGH)
    first = (place * 2 + core) * owned
    new_basis = (
        lax.dynamic_slice_in_dim(coefficients, first, owned, 0)
        * lax.dynamic_slice_in_dim(scale, first, owned, 0)[:, None]
    )
    new_weights = (weights.astype(jnp.float32) - step_size * math.sqrt(D / FF) * update).astype(
        jnp.bfloat16
    )
    return (new_weights, new_momentum, new_basis)


def solution(mesh):
    devices = mesh.devices
    split = Mesh(
        devices.reshape(4, devices.shape[0] // 8, 2, 4, devices.shape[1] // 4),
        ("far", "near", "core", "x", "y"),
    )
    spec = P(("far", "near", "core"), ("x", "y"))
    return jax.shard_map(
        on_device, mesh=split, in_specs=(spec,) * 4, out_specs=(spec,) * 3, check_vma=False
    )
```

```python
import functools
import math

import jax
import jax.numpy as jnp
from jax import lax
from jax.experimental import pallas as pl
from jax.experimental.pallas import tpu as pltpu
from jax.sharding import Mesh, PartitionSpec as P

D = 8192
FF = 14336

momentum_decay = 0.95
step_size = 2.0
epsilon = 1e-06

DEPTH = ("far", "near")
COLUMN_BLOCKS = ("x", "y")
HIGH = lax.Precision.HIGH
SWAP = [(0, 1), (1, 0)]


def dot(left_side, right_side, contract_left, contract_right, precision=lax.Precision.HIGHEST):
    return lax.dot_general(
        left_side,
        right_side,
        (((contract_left,), (contract_right,)), ((), ())),
        precision=precision,
        preferred_element_type=jnp.float32,
    )


def exchange(array, axes):
    return lax.all_to_all(array, axes, 0, 0, tiled=True)


def spread(array, axes, count):
    return exchange(
        jnp.broadcast_to(array[None], (count,) + array.shape).reshape(
            (count * array.shape[0],) + array.shape[1:]
        ),
        axes,
    )


SUB = 8
TILE = 128
GROUP = 32


def factor_step(work, wide, at, block):
    lane = lax.broadcasted_iota(jnp.int32,(SUB,TILE),1)
    sub = lax.broadcasted_iota(jnp.int32,(SUB,TILE),0)
    own = (lane>=at)&(lane<at+SUB)
    for j in range(SUB):
        wide[j] = jnp.broadcast_to(block[:,at+j:at+j+1],(SUB,TILE))
    work[at:at+SUB,:] = jnp.where(own, jnp.where(lane-at==sub,1.0,0.0), block)
    spread = lambda ref_row: jnp.broadcast_to(ref_row,(SUB,TILE))
    gram = [[spread(wide[j,i:i+1,:]) for j in range(i+1)] for i in range(SUB)]
    low = [[None]*SUB for _ in range(SUB)]
    inv = [None]*SUB
    rows = [None]*SUB
    for j in range(SUB):
        inv[j] = lax.rsqrt(gram[j][j])
        for i in range(j+1,SUB):
            low[i][j] = gram[i][j]*inv[j]
        for i in range(j+1,SUB):
            for m in range(j+1,i+1):
                gram[i][m] = gram[i][m]-low[i][j]*low[m][j]
        row = spread(work[at+j:at+j+1,:])
        for m in range(j):
            row = row - low[j][m]*rows[m]
        rows[j] = row*inv[j]
    out = rows[SUB-1]
    for i in range(SUB-1):
        out = jnp.where(sub==i, rows[i], out)
    work[at:at+SUB,:] = out
    far = (at//GROUP+2)*GROUP
    ahead = None
    for nxt in range(at+SUB, min(far,TILE), SUB):
        block = work[nxt:nxt+SUB,:]
        left=[]
        total = jnp.where(own,0.0,block)
        for j in range(SUB):
            col = jnp.broadcast_to(block[:,at+j:at+j+1],(SUB,TILE))
            for m in range(j):
                col = col - left[m]*low[j][m]
            left.append(col*inv[j])
            total = total - left[j]*rows[j]
        if nxt == at+SUB:
            ahead = total
        else:
            work[nxt:nxt+SUB,:] = total
    return ahead


def group_step(work, at):
    far = at+2*GROUP
    if far < TILE:
        rows = work[at:at+GROUP,:]
        lane = lax.broadcasted_iota(jnp.int32,(GROUP,TILE),1)-at
        sub = lax.broadcasted_iota(jnp.int32,(GROUP,TILE),0)
        clean = jnp.where((lane>=sub//SUB*SUB+SUB)&(lane<GROUP),0.0,rows)
        prod = dot(rows,clean,0,0)
        rest = work[far:,:]
        lanes = lax.broadcasted_iota(jnp.int32,rest.shape,1)
        work[far:,:] = jnp.where((lanes>=at)&(lanes<at+GROUP),0.0,rest) - prod[far:,:]


def inverse_factor_kernel(
    core_ref, own_ref, other_ref, out_ref, zero_ref, work, wide, *, owned
):
    n = out_ref.shape[0]
    tiles = n//TILE
    core = core_ref[0]
    for t in range(n // (2 * owned)):
        first = pl.multiple_of(2 * t * owned + core * owned, owned)
        second = pl.multiple_of(2 * t * owned + (1 - core) * owned, owned)
        out_ref[pl.ds(first, owned), :] = own_ref[t*owned:(t+1)*owned, :]
        out_ref[pl.ds(second, owned), :] = other_ref[t*owned:(t+1)*owned, :]
    def panel(p, carry):
        at = pl.multiple_of(p*TILE,TILE)
        work[...] = out_ref[pl.ds(at,TILE),pl.ds(at,TILE)]
        block = work[0:SUB,:]
        for k in range(TILE//SUB):
            block = factor_step(work, wide.at[k%2], k*SUB, block)
            if (k+1)*SUB%GROUP==0:
                group_step(work,(k+1)*SUB-GROUP)
        r = lax.broadcasted_iota(jnp.int32,(TILE,TILE),0); c = lax.broadcasted_iota(jnp.int32,(TILE,TILE),1)
        inverse = jnp.where(r>=c, work[...], 0.0)
        out_ref[pl.ds(at,TILE),pl.ds(at,TILE)] = jnp.where(r==c,1.0,0.0)
        new = dot(inverse, out_ref[pl.ds(at,TILE),:],1,0)
        out_ref[pl.ds(at,TILE),:] = new
        for q in range(1,tiles):
            @pl.when(q>p)
            def _():
                out_ref[q*TILE:(q+1)*TILE,pl.ds(at,TILE)] = jnp.zeros((TILE,TILE),jnp.float32)
                out_ref[q*TILE:(q+1)*TILE,:] = out_ref[q*TILE:(q+1)*TILE,:] - dot(new[:,q*TILE:(q+1)*TILE],new,0,0)
        return carry
    lax.fori_loop(0,tiles,panel,0)
    for q in range(tiles-1):
        out_ref[q*TILE:(q+1)*TILE,(q+1)*TILE:] = jnp.zeros((TILE,n-(q+1)*TILE),jnp.float32)
    zero_ref[...] = jnp.zeros_like(zero_ref)

def inverse_factor(core, own, other, owned, columns):
    size = own.shape[1]
    whole = pl.BlockSpec(memory_space=pltpu.VMEM)
    return pl.pallas_call(
        functools.partial(inverse_factor_kernel, owned=owned),
        out_shape=(
            jax.ShapeDtypeStruct((size, size), jnp.float32),
            jax.ShapeDtypeStruct((owned, columns), jnp.float32),
        ),
        in_specs=[pl.BlockSpec(memory_space=pltpu.SMEM), whole, whole],
        out_specs=(whole, whole),
        scratch_shapes=[
            pltpu.VMEM((TILE, TILE), jnp.float32),
            pltpu.VMEM((2, SUB, SUB, TILE), jnp.float32),
        ],
        cost_estimate=pl.CostEstimate(
            flops=200_000_000, bytes_accessed=4 * size * size * 2, transcendentals=size
        ),
        compiler_params=pltpu.CompilerParams(vmem_limit_bytes=8 * 2**20),
        name="inverse_factor",
    )(core.reshape(1), own, other)


def total(array, count):
    return jnp.sum(array.reshape((count, array.shape[0] // count) + array.shape[1:]), axis=0)


def by_core(core, own, other, axis):
    return jnp.where(
        core == 0, jnp.concatenate([own, other], axis), jnp.concatenate([other, own], axis)
    )


def one_side(rank, owned, core):
    ranks = lax.broadcasted_iota(jnp.int32, (rank, rank // 2), 0)
    kept = lax.broadcasted_iota(jnp.int32, (rank, rank // 2), 1)
    source = (kept // owned * 2 + core) * owned + kept % owned
    return (ranks == source).astype(jnp.float32)


def on_device(weights, momentum, gradient, warm_basis):
    rows, columns = momentum.shape
    owned = warm_basis.shape[0]
    depth = lax.axis_size(DEPTH)
    blocks = lax.axis_size(COLUMN_BLOCKS)
    far, near = lax.axis_size("far"), lax.axis_size("near")
    rank = owned * depth * 2
    half = rank // 2
    core = lax.axis_index("core")
    place = lax.axis_index(DEPTH)

    blended = momentum + gradient.astype(jnp.float32)
    partner = lax.ppermute(blended, "core", SWAP)
    basis = lax.all_gather(warm_basis, DEPTH, axis=0, tiled=True)
    partial = jnp.concatenate([dot(blended, basis, 1, 1), dot(partner, basis, 1, 1)])
    part = total(exchange(partial, COLUMN_BLOCKS), blocks)
    projected = spread(part, COLUMN_BLOCKS, blocks)
    others = lax.ppermute(projected, "core", SWAP)
    others = jnp.concatenate([others[rows:], others[:rows]])

    moved = dot(projected[:rows], blended, 0, 0, HIGH) + dot(
        projected[rows:], partner, 0, 0, HIGH
    )
    moved = lax.psum_scatter(moved, DEPTH, scatter_dimension=0, tiled=True)

    kept = lax.broadcasted_iota(jnp.int32, (rank, rank), 0)
    ranks = lax.broadcasted_iota(jnp.int32, (rank, rank), 1)
    source = ranks // owned % 2 * half + ranks // (2 * owned) * owned + ranks % owned
    order = (kept == source).astype(jnp.float32)

    share = half // blocks
    picked = lax.dynamic_slice_in_dim(
        projected, lax.axis_index(COLUMN_BLOCKS) * share, share, 1
    )
    same = dot(picked, projected, 0, 0)
    cross = dot(picked, others, 0, 0)
    gram = dot(by_core(core, same, cross, 1), order, 1, 0)
    gram = total(spread(gram, "far", far), far)
    gram = total(spread(gram, "near", near), near)
    gram = spread(gram, COLUMN_BLOCKS, blocks)
    inverse, zero = inverse_factor(
        core, gram, lax.ppermute(gram, "core", SWAP), owned, columns
    )

    moved = lax.all_gather(moved + zero, DEPTH, axis=0, tiled=True)
    handed = lax.ppermute(moved, "core", SWAP)
    inverse_own = dot(inverse, one_side(rank, owned, core), 1, 0, HIGH)
    inverse_other = dot(inverse, one_side(rank, owned, 1 - core), 1, 0, HIGH)
    orthonormal = dot(projected[:rows], inverse_own, 1, 1, HIGH) + dot(
        others[:rows], inverse_other, 1, 1, HIGH
    )
    coefficients = dot(inverse_own, moved, 1, 0, HIGH) + dot(inverse_other, handed, 1, 0, HIGH)
    energy = jnp.sum(coefficients * coefficients, axis=1).reshape(rank // 128, 128)
    energy = total(spread(energy, COLUMN_BLOCKS, blocks), blocks).reshape(rank)
    scale = lax.rsqrt(energy / FF + epsilon)
    feedback = dot(orthonormal, coefficients, 1, 0, HIGH)
    new_momentum = blended - (1.0 - momentum_decay) * feedback
    update = dot(orthonormal * scale[None, :], coefficients, 1, 0, HIGH)
    first = (place * 2 + core) * owned
    new_basis = (
        lax.dynamic_slice_in_dim(coefficients, first, owned, 0)
        * lax.dynamic_slice_in_dim(scale, first, owned, 0)[:, None]
    )
    new_weights = (weights.astype(jnp.float32) - step_size * math.sqrt(D / FF) * update).astype(
        jnp.bfloat16
    )
    return (new_weights, new_momentum, new_basis)


def solution(mesh):
    devices = mesh.devices
    split = Mesh(
        devices.reshape(4, devices.shape[0] // 8, 2, 4, devices.shape[1] // 4),
        ("far", "near", "core", "x", "y"),
    )
    spec = P(("far", "near", "core"), ("x", "y"))
    return jax.shard_map(
        on_device, mesh=split, in_specs=(spec,) * 4, out_specs=(spec,) * 3, check_vma=False
    )
```

```python
import functools
import math

import jax
import jax.numpy as jnp
from jax import lax
from jax.experimental import pallas as pl
from jax.experimental.pallas import tpu as pltpu
from jax.sharding import Mesh, PartitionSpec as P

D = 8192
FF = 14336

momentum_decay = 0.95
step_size = 2.0
epsilon = 1e-06

DEPTH = ("far", "near")
COLUMN_BLOCKS = ("x", "y")
HIGH = lax.Precision.HIGH
SWAP = [(0, 1), (1, 0)]


def dot(left_side, right_side, contract_left, contract_right, precision=lax.Precision.HIGHEST):
    return lax.dot_general(
        left_side,
        right_side,
        (((contract_left,), (contract_right,)), ((), ())),
        precision=precision,
        preferred_element_type=jnp.float32,
    )


def exchange(array, axes):
    return lax.all_to_all(array, axes, 0, 0, tiled=True)


def spread(array, axes, count):
    return exchange(
        jnp.broadcast_to(array[None], (count,) + array.shape).reshape(
            (count * array.shape[0],) + array.shape[1:]
        ),
        axes,
    )


SUB = 8
TILE = 128
GROUP = 32


def factor_step(work, wide, at, block):
    lane = lax.broadcasted_iota(jnp.int32,(SUB,TILE),1)
    sub = lax.broadcasted_iota(jnp.int32,(SUB,TILE),0)
    own = (lane>=at)&(lane<at+SUB)
    for j in range(SUB):
        wide[j] = jnp.broadcast_to(block[:,at+j:at+j+1],(SUB,TILE))
    work[at:at+SUB,:] = jnp.where(own, jnp.where(lane-at==sub,1.0,0.0), block)
    spread = lambda ref_row: jnp.broadcast_to(ref_row,(SUB,TILE))
    gram = [[spread(wide[j,i:i+1,:]) for j in range(i+1)] for i in range(SUB)]
    low = [[None]*SUB for _ in range(SUB)]
    inv = [None]*SUB
    rows = [None]*SUB
    for j in range(SUB):
        inv[j] = lax.rsqrt(gram[j][j])
        for i in range(j+1,SUB):
            low[i][j] = gram[i][j]*inv[j]
        for i in range(j+1,SUB):
            for m in range(j+1,i+1):
                gram[i][m] = gram[i][m]-low[i][j]*low[m][j]
        row = spread(work[at+j:at+j+1,:])
        for m in range(j):
            row = row - low[j][m]*rows[m]
        rows[j] = row*inv[j]
    out = rows[SUB-1]
    for i in range(SUB-1):
        out = jnp.where(sub==i, rows[i], out)
    work[at:at+SUB,:] = out
    far = (at//GROUP+2)*GROUP
    ahead = None
    for nxt in range(at+SUB, min(far,TILE), SUB):
        block = work[nxt:nxt+SUB,:]
        left=[]
        total = jnp.where(own,0.0,block)
        for j in range(SUB):
            col = jnp.broadcast_to(block[:,at+j:at+j+1],(SUB,TILE))
            for m in range(j):
                col = col - left[m]*low[j][m]
            left.append(col*inv[j])
            total = total - left[j]*rows[j]
        if nxt == at+SUB:
            ahead = total
        else:
            work[nxt:nxt+SUB,:] = total
    return ahead


def group_step(work, at):
    far = at+2*GROUP
    if far < TILE:
        rows = work[at:at+GROUP,:]
        lane = lax.broadcasted_iota(jnp.int32,(GROUP,TILE),1)-at
        sub = lax.broadcasted_iota(jnp.int32,(GROUP,TILE),0)
        clean = jnp.where((lane>=sub//SUB*SUB+SUB)&(lane<GROUP),0.0,rows)
        prod = dot(rows,clean,0,0)
        rest = work[far:,:]
        lanes = lax.broadcasted_iota(jnp.int32,rest.shape,1)
        work[far:,:] = jnp.where((lanes>=at)&(lanes<at+GROUP),0.0,rest) - prod[far:,:]


def inverse_factor_kernel(
    core_ref, own_ref, other_ref, out_ref, zero_ref, work, wide, *, owned
):
    n = out_ref.shape[0]
    tiles = n//TILE
    core = core_ref[0]
    for t in range(n // (2 * owned)):
        first = pl.multiple_of(2 * t * owned + core * owned, owned)
        second = pl.multiple_of(2 * t * owned + (1 - core) * owned, owned)
        out_ref[pl.ds(first, owned), :] = own_ref[t*owned:(t+1)*owned, :]
        out_ref[pl.ds(second, owned), :] = other_ref[t*owned:(t+1)*owned, :]
    def panel(p, carry):
        at = pl.multiple_of(p*TILE,TILE)
        work[...] = out_ref[pl.ds(at,TILE),pl.ds(at,TILE)]
        block = work[0:SUB,:]
        for k in range(TILE//SUB):
            block = factor_step(work, wide.at[k%2], k*SUB, block)
            if (k+1)*SUB%GROUP==0:
                group_step(work,(k+1)*SUB-GROUP)
        r = lax.broadcasted_iota(jnp.int32,(TILE,TILE),0); c = lax.broadcasted_iota(jnp.int32,(TILE,TILE),1)
        inverse = jnp.where(r>=c, work[...], 0.0)
        out_ref[pl.ds(at,TILE),pl.ds(at,TILE)] = jnp.where(r==c,1.0,0.0)
        new = dot(inverse, out_ref[pl.ds(at,TILE),:],1,0)
        out_ref[pl.ds(at,TILE),:] = new
        for q in range(1,tiles):
            @pl.when(q>p)
            def _():
                out_ref[q*TILE:(q+1)*TILE,pl.ds(at,TILE)] = jnp.zeros((TILE,TILE),jnp.float32)
                out_ref[q*TILE:(q+1)*TILE,:] = out_ref[q*TILE:(q+1)*TILE,:] - dot(new[:,q*TILE:(q+1)*TILE],new,0,0)
        return carry
    lax.fori_loop(0,tiles,panel,0)
    for q in range(tiles-1):
        out_ref[q*TILE:(q+1)*TILE,(q+1)*TILE:] = jnp.zeros((TILE,n-(q+1)*TILE),jnp.float32)
    zero_ref[...] = jnp.zeros_like(zero_ref)

def inverse_factor(core, own, other, owned, columns):
    size = own.shape[1]
    whole = pl.BlockSpec(memory_space=pltpu.VMEM)
    return pl.pallas_call(
        functools.partial(inverse_factor_kernel, owned=owned),
        out_shape=(
            jax.ShapeDtypeStruct((size, size), jnp.float32),
            jax.ShapeDtypeStruct((owned, columns), jnp.float32),
        ),
        in_specs=[pl.BlockSpec(memory_space=pltpu.SMEM), whole, whole],
        out_specs=(whole, whole),
        scratch_shapes=[
            pltpu.VMEM((TILE, TILE), jnp.float32),
            pltpu.VMEM((2, SUB, SUB, TILE), jnp.float32),
        ],
        cost_estimate=pl.CostEstimate(
            flops=200_000_000, bytes_accessed=4 * size * size * 2, transcendentals=size
        ),
        compiler_params=pltpu.CompilerParams(vmem_limit_bytes=8 * 2**20),
        name="inverse_factor",
    )(core.reshape(1), own, other)


def total(array, count):
    return jnp.sum(array.reshape((count, array.shape[0] // count) + array.shape[1:]), axis=0)


def by_core(core, own, other, axis):
    return jnp.where(
        core == 0, jnp.concatenate([own, other], axis), jnp.concatenate([other, own], axis)
    )


def one_side(rank, owned, core):
    ranks = lax.broadcasted_iota(jnp.int32, (rank, rank // 2), 0)
    kept = lax.broadcasted_iota(jnp.int32, (rank, rank // 2), 1)
    source = (kept // owned * 2 + core) * owned + kept % owned
    return (ranks == source).astype(jnp.float32)


def finish_kernel(
    first_ref, energy_ref, orthonormal_ref, coefficients_ref, weights_ref, out_ref, basis_ref
):
    owned = basis_ref.shape[0]
    energy = jnp.sum(energy_ref[...], axis=0)
    scale = lax.rsqrt(energy / FF + epsilon)
    scale = jnp.concatenate([scale[i : i + 1] for i in range(scale.shape[0])], axis=1)
    coefficients = coefficients_ref[...]
    row = lax.broadcasted_iota(jnp.int32, (owned, scale.shape[1]), 0) + first_ref[0]
    column = lax.broadcasted_iota(jnp.int32, (owned, scale.shape[1]), 1)
    own = jnp.sum(jnp.where(row == column, scale, 0.0), axis=1, keepdims=True)
    basis_ref[...] = coefficients_ref[pl.ds(pl.multiple_of(first_ref[0], owned), owned), :] * own
    update = dot(orthonormal_ref[...] * scale, coefficients, 1, 0, HIGH)
    out_ref[...] = (
        weights_ref[...].astype(jnp.float32) - step_size * math.sqrt(D / FF) * update
    ).astype(jnp.bfloat16)


def finish(first, energy, orthonormal, coefficients, weights, owned):
    whole = pl.BlockSpec(memory_space=pltpu.VMEM)
    rows, columns = weights.shape
    return pl.pallas_call(
        finish_kernel,
        out_shape=(
            jax.ShapeDtypeStruct((rows, columns), jnp.bfloat16),
            jax.ShapeDtypeStruct((owned, columns), jnp.float32),
        ),
        in_specs=[pl.BlockSpec(memory_space=pltpu.SMEM), whole, whole, whole, whole],
        out_specs=(whole, whole),
        cost_estimate=pl.CostEstimate(
            flops=6 * rows * columns * coefficients.shape[0],
            bytes_accessed=4 * rows * columns,
            transcendentals=512,
        ),
        compiler_params=pltpu.CompilerParams(vmem_limit_bytes=24 * 2**20),
        name="finish",
    )(first.reshape(1), energy, orthonormal, coefficients, weights)


def on_device(weights, momentum, gradient, warm_basis):
    rows, columns = momentum.shape
    owned = warm_basis.shape[0]
    depth = lax.axis_size(DEPTH)
    blocks = lax.axis_size(COLUMN_BLOCKS)
    far, near = lax.axis_size("far"), lax.axis_size("near")
    rank = owned * depth * 2
    half = rank // 2
    core = lax.axis_index("core")
    place = lax.axis_index(DEPTH)

    blended = momentum + gradient.astype(jnp.float32)
    partner = lax.ppermute(blended, "core", SWAP)
    basis = lax.all_gather(warm_basis, DEPTH, axis=0, tiled=True)
    partial = jnp.concatenate([dot(blended, basis, 1, 1), dot(partner, basis, 1, 1)])
    part = total(exchange(partial, COLUMN_BLOCKS), blocks)
    projected = spread(part, COLUMN_BLOCKS, blocks)
    others = lax.ppermute(projected, "core", SWAP)
    others = jnp.concatenate([others[rows:], others[:rows]])

    moved = dot(projected[:rows], blended, 0, 0, HIGH) + dot(
        projected[rows:], partner, 0, 0, HIGH
    )
    moved = lax.psum_scatter(moved, DEPTH, scatter_dimension=0, tiled=True)

    kept = lax.broadcasted_iota(jnp.int32, (rank, rank), 0)
    ranks = lax.broadcasted_iota(jnp.int32, (rank, rank), 1)
    source = ranks // owned % 2 * half + ranks // (2 * owned) * owned + ranks % owned
    order = (kept == source).astype(jnp.float32)

    share = half // blocks
    picked = lax.dynamic_slice_in_dim(
        projected, lax.axis_index(COLUMN_BLOCKS) * share, share, 1
    )
    same = dot(picked, projected, 0, 0)
    cross = dot(picked, others, 0, 0)
    gram = dot(by_core(core, same, cross, 1), order, 1, 0)
    gram = total(spread(gram, "far", far), far)
    gram = total(spread(gram, "near", near), near)
    gram = spread(gram, COLUMN_BLOCKS, blocks)
    inverse, zero = inverse_factor(
        core, gram, lax.ppermute(gram, "core", SWAP), owned, columns
    )

    moved = lax.all_gather(moved + zero, DEPTH, axis=0, tiled=True)
    handed = lax.ppermute(moved, "core", SWAP)
    inverse_own = dot(inverse, one_side(rank, owned, core), 1, 0, HIGH)
    inverse_other = dot(inverse, one_side(rank, owned, 1 - core), 1, 0, HIGH)
    orthonormal = dot(projected[:rows], inverse_own, 1, 1, HIGH) + dot(
        others[:rows], inverse_other, 1, 1, HIGH
    )
    coefficients = dot(inverse_own, moved, 1, 0, HIGH) + dot(inverse_other, handed, 1, 0, HIGH)
    energy = jnp.sum(coefficients * coefficients, axis=1).reshape(rank // 128, 128)
    energy = spread(energy, COLUMN_BLOCKS, blocks).reshape(blocks, rank // 128, 128)
    feedback = dot(orthonormal, coefficients, 1, 0, HIGH)
    new_momentum = blended - (1.0 - momentum_decay) * feedback
    first = (place * 2 + core) * owned
    new_weights, new_basis = finish(first, energy, orthonormal, coefficients, weights, owned)
    return (new_weights, new_momentum, new_basis)


def solution(mesh):
    devices = mesh.devices
    split = Mesh(
        devices.reshape(4, devices.shape[0] // 8, 2, 4, devices.shape[1] // 4),
        ("far", "near", "core", "x", "y"),
    )
    spec = P(("far", "near", "core"), ("x", "y"))
    return jax.shard_map(
        on_device, mesh=split, in_specs=(spec,) * 4, out_specs=(spec,) * 3, check_vma=False
    )
```

```python
import functools
import math

import jax
import jax.numpy as jnp
from jax import lax
from jax.experimental import pallas as pl
from jax.experimental.pallas import tpu as pltpu
from jax.sharding import Mesh, PartitionSpec as P

D = 8192
FF = 14336

momentum_decay = 0.95
step_size = 2.0
epsilon = 1e-06

DEPTH = ("far", "near")
COLUMN_BLOCKS = ("x", "y")
HIGH = lax.Precision.HIGH
SWAP = [(0, 1), (1, 0)]


def dot(left_side, right_side, contract_left, contract_right, precision=lax.Precision.HIGHEST):
    return lax.dot_general(
        left_side,
        right_side,
        (((contract_left,), (contract_right,)), ((), ())),
        precision=precision,
        preferred_element_type=jnp.float32,
    )


def exchange(array, axes):
    return lax.all_to_all(array, axes, 0, 0, tiled=True)


def spread(array, axes, count):
    return exchange(
        jnp.broadcast_to(array[None], (count,) + array.shape).reshape(
            (count * array.shape[0],) + array.shape[1:]
        ),
        axes,
    )


SUB = 8
TILE = 128
GROUP = 32


def factor_step(work, wide, at, block):
    lane = lax.broadcasted_iota(jnp.int32,(SUB,TILE),1)
    sub = lax.broadcasted_iota(jnp.int32,(SUB,TILE),0)
    own = (lane>=at)&(lane<at+SUB)
    for j in range(SUB):
        wide[j] = jnp.broadcast_to(block[:,at+j:at+j+1],(SUB,TILE))
    work[at:at+SUB,:] = jnp.where(own, jnp.where(lane-at==sub,1.0,0.0), block)
    spread = lambda ref_row: jnp.broadcast_to(ref_row,(SUB,TILE))
    gram = [[spread(wide[j,i:i+1,:]) for j in range(i+1)] for i in range(SUB)]
    low = [[None]*SUB for _ in range(SUB)]
    inv = [None]*SUB
    rows = [None]*SUB
    for j in range(SUB):
        inv[j] = lax.rsqrt(gram[j][j])
        for i in range(j+1,SUB):
            low[i][j] = gram[i][j]*inv[j]
        for i in range(j+1,SUB):
            for m in range(j+1,i+1):
                gram[i][m] = gram[i][m]-low[i][j]*low[m][j]
        row = spread(work[at+j:at+j+1,:])
        for m in range(j):
            row = row - low[j][m]*rows[m]
        rows[j] = row*inv[j]
    out = rows[SUB-1]
    for i in range(SUB-1):
        out = jnp.where(sub==i, rows[i], out)
    work[at:at+SUB,:] = out
    far = (at//GROUP+2)*GROUP
    ahead = None
    for nxt in range(at+SUB, min(far,TILE), SUB):
        block = work[nxt:nxt+SUB,:]
        left=[]
        total = jnp.where(own,0.0,block)
        for j in range(SUB):
            col = jnp.broadcast_to(block[:,at+j:at+j+1],(SUB,TILE))
            for m in range(j):
                col = col - left[m]*low[j][m]
            left.append(col*inv[j])
            total = total - left[j]*rows[j]
        if nxt == at+SUB:
            ahead = total
        else:
            work[nxt:nxt+SUB,:] = total
    return ahead


def group_step(work, at):
    far = at+2*GROUP
    if far < TILE:
        rows = work[at:at+GROUP,:]
        lane = lax.broadcasted_iota(jnp.int32,(GROUP,TILE),1)-at
        sub = lax.broadcasted_iota(jnp.int32,(GROUP,TILE),0)
        clean = jnp.where((lane>=sub//SUB*SUB+SUB)&(lane<GROUP),0.0,rows)
        prod = dot(rows,clean,0,0)
        rest = work[far:,:]
        lanes = lax.broadcasted_iota(jnp.int32,rest.shape,1)
        work[far:,:] = jnp.where((lanes>=at)&(lanes<at+GROUP),0.0,rest) - prod[far:,:]


def inverse_factor_kernel(
    core_ref, own_ref, other_ref, out_ref, zero_ref, work, wide, *, owned
):
    n = out_ref.shape[0]
    tiles = n//TILE
    core = core_ref[0]
    for t in range(n // (2 * owned)):
        first = pl.multiple_of(2 * t * owned + core * owned, owned)
        second = pl.multiple_of(2 * t * owned + (1 - core) * owned, owned)
        out_ref[pl.ds(first, owned), :] = own_ref[t*owned:(t+1)*owned, :]
        out_ref[pl.ds(second, owned), :] = other_ref[t*owned:(t+1)*owned, :]
    def panel(p, carry):
        at = pl.multiple_of(p*TILE,TILE)
        work[...] = out_ref[pl.ds(at,TILE),pl.ds(at,TILE)]
        block = work[0:SUB,:]
        for k in range(TILE//SUB):
            block = factor_step(work, wide.at[k%2], k*SUB, block)
            if (k+1)*SUB%GROUP==0:
                group_step(work,(k+1)*SUB-GROUP)
        r = lax.broadcasted_iota(jnp.int32,(TILE,TILE),0); c = lax.broadcasted_iota(jnp.int32,(TILE,TILE),1)
        inverse = jnp.where(r>=c, work[...], 0.0)
        out_ref[pl.ds(at,TILE),pl.ds(at,TILE)] = jnp.where(r==c,1.0,0.0)
        new = dot(inverse, out_ref[pl.ds(at,TILE),:],1,0)
        out_ref[pl.ds(at,TILE),:] = new
        for q in range(1,tiles):
            @pl.when(q>p)
            def _():
                out_ref[q*TILE:(q+1)*TILE,pl.ds(at,TILE)] = jnp.zeros((TILE,TILE),jnp.float32)
                out_ref[q*TILE:(q+1)*TILE,:] = out_ref[q*TILE:(q+1)*TILE,:] - dot(new[:,q*TILE:(q+1)*TILE],new,0,0)
        return carry
    lax.fori_loop(0,tiles,panel,0)
    for q in range(tiles-1):
        out_ref[q*TILE:(q+1)*TILE,(q+1)*TILE:] = jnp.zeros((TILE,n-(q+1)*TILE),jnp.float32)
    zero_ref[...] = jnp.zeros_like(zero_ref)

def inverse_factor(core, own, other, owned, columns):
    size = own.shape[1]
    whole = pl.BlockSpec(memory_space=pltpu.VMEM)
    return pl.pallas_call(
        functools.partial(inverse_factor_kernel, owned=owned),
        out_shape=(
            jax.ShapeDtypeStruct((size, size), jnp.float32),
            jax.ShapeDtypeStruct((owned, columns), jnp.float32),
        ),
        in_specs=[pl.BlockSpec(memory_space=pltpu.SMEM), whole, whole],
        out_specs=(whole, whole),
        scratch_shapes=[
            pltpu.VMEM((TILE, TILE), jnp.float32),
            pltpu.VMEM((2, SUB, SUB, TILE), jnp.float32),
        ],
        cost_estimate=pl.CostEstimate(
            flops=200_000_000, bytes_accessed=4 * size * size * 2, transcendentals=size
        ),
        compiler_params=pltpu.CompilerParams(vmem_limit_bytes=8 * 2**20),
        name="inverse_factor",
    )(core.reshape(1), own, other)


def total(array, count):
    return jnp.sum(array.reshape((count, array.shape[0] // count) + array.shape[1:]), axis=0)


def by_core(core, own, other, axis):
    return jnp.where(
        core == 0, jnp.concatenate([own, other], axis), jnp.concatenate([other, own], axis)
    )


def one_side(rank, owned, core):
    ranks = lax.broadcasted_iota(jnp.int32, (rank, rank // 2), 0)
    kept = lax.broadcasted_iota(jnp.int32, (rank, rank // 2), 1)
    source = (kept // owned * 2 + core) * owned + kept % owned
    return (ranks == source).astype(jnp.float32)


def finish_kernel(
    first_ref,
    energy_ref,
    orthonormal_ref,
    coefficients_ref,
    weights_ref,
    blended_ref,
    out_ref,
    basis_ref,
    momentum_ref,
):
    owned = basis_ref.shape[0]
    energy = jnp.sum(energy_ref[...], axis=0)
    scale = lax.rsqrt(energy / FF + epsilon)
    scale = jnp.concatenate([scale[i : i + 1] for i in range(scale.shape[0])], axis=1)
    coefficients = coefficients_ref[...]
    row = lax.broadcasted_iota(jnp.int32, (owned, scale.shape[1]), 0) + first_ref[0]
    column = lax.broadcasted_iota(jnp.int32, (owned, scale.shape[1]), 1)
    own = jnp.sum(jnp.where(row == column, scale, 0.0), axis=1, keepdims=True)
    basis_ref[...] = coefficients_ref[pl.ds(pl.multiple_of(first_ref[0], owned), owned), :] * own
    orthonormal = orthonormal_ref[...]
    rows = orthonormal.shape[0]
    both = dot(jnp.concatenate([orthonormal * scale, orthonormal]), coefficients, 1, 0, HIGH)
    update = both[:rows]
    momentum_ref[...] = blended_ref[...] - (1.0 - momentum_decay) * both[rows:]
    out_ref[...] = (
        weights_ref[...].astype(jnp.float32) - step_size * math.sqrt(D / FF) * update
    ).astype(jnp.bfloat16)


def finish(first, energy, orthonormal, coefficients, weights, blended, owned):
    whole = pl.BlockSpec(memory_space=pltpu.VMEM)
    rows, columns = weights.shape
    return pl.pallas_call(
        finish_kernel,
        out_shape=(
            jax.ShapeDtypeStruct((rows, columns), jnp.bfloat16),
            jax.ShapeDtypeStruct((owned, columns), jnp.float32),
            jax.ShapeDtypeStruct((rows, columns), jnp.float32),
        ),
        in_specs=[pl.BlockSpec(memory_space=pltpu.SMEM)] + [whole] * 5,
        out_specs=(whole,) * 3,
        cost_estimate=pl.CostEstimate(
            flops=6 * rows * columns * coefficients.shape[0],
            bytes_accessed=4 * rows * columns,
            transcendentals=512,
        ),
        compiler_params=pltpu.CompilerParams(vmem_limit_bytes=24 * 2**20),
        name="finish",
    )(first.reshape(1), energy, orthonormal, coefficients, weights, blended)


def on_device(weights, momentum, gradient, warm_basis):
    rows, columns = momentum.shape
    owned = warm_basis.shape[0]
    depth = lax.axis_size(DEPTH)
    blocks = lax.axis_size(COLUMN_BLOCKS)
    far, near = lax.axis_size("far"), lax.axis_size("near")
    rank = owned * depth * 2
    half = rank // 2
    core = lax.axis_index("core")
    place = lax.axis_index(DEPTH)

    blended = momentum + gradient.astype(jnp.float32)
    partner = lax.ppermute(blended, "core", SWAP)
    basis = lax.all_gather(warm_basis, DEPTH, axis=0, tiled=True)
    partial = jnp.concatenate([dot(blended, basis, 1, 1), dot(partner, basis, 1, 1)])
    part = total(exchange(partial, COLUMN_BLOCKS), blocks)
    projected = spread(part, COLUMN_BLOCKS, blocks)
    others = lax.ppermute(projected, "core", SWAP)
    others = jnp.concatenate([others[rows:], others[:rows]])

    moved = dot(projected[:rows], blended, 0, 0, HIGH) + dot(
        projected[rows:], partner, 0, 0, HIGH
    )
    moved = lax.psum_scatter(moved, DEPTH, scatter_dimension=0, tiled=True)

    kept = lax.broadcasted_iota(jnp.int32, (rank, rank), 0)
    ranks = lax.broadcasted_iota(jnp.int32, (rank, rank), 1)
    source = ranks // owned % 2 * half + ranks // (2 * owned) * owned + ranks % owned
    order = (kept == source).astype(jnp.float32)

    share = half // blocks
    picked = lax.dynamic_slice_in_dim(
        projected, lax.axis_index(COLUMN_BLOCKS) * share, share, 1
    )
    same = dot(picked, projected, 0, 0)
    cross = dot(picked, others, 0, 0)
    gram = dot(by_core(core, same, cross, 1), order, 1, 0)
    gram = total(spread(gram, "far", far), far)
    gram = total(spread(gram, "near", near), near)
    gram = spread(gram, COLUMN_BLOCKS, blocks)
    inverse, zero = inverse_factor(
        core, gram, lax.ppermute(gram, "core", SWAP), owned, columns
    )

    moved = lax.all_gather(moved + zero, DEPTH, axis=0, tiled=True)
    handed = lax.ppermute(moved, "core", SWAP)
    inverse_own = dot(inverse, one_side(rank, owned, core), 1, 0, HIGH)
    inverse_other = dot(inverse, one_side(rank, owned, 1 - core), 1, 0, HIGH)
    orthonormal = dot(projected[:rows], inverse_own, 1, 1, HIGH) + dot(
        others[:rows], inverse_other, 1, 1, HIGH
    )
    coefficients = dot(inverse_own, moved, 1, 0, HIGH) + dot(inverse_other, handed, 1, 0, HIGH)
    energy = jnp.sum(coefficients * coefficients, axis=1).reshape(rank // 128, 128)
    energy = spread(energy, COLUMN_BLOCKS, blocks).reshape(blocks, rank // 128, 128)
    first = (place * 2 + core) * owned
    new_weights, new_basis, new_momentum = finish(
        first, energy, orthonormal, coefficients, weights, blended, owned
    )
    return (new_weights, new_momentum, new_basis)


def solution(mesh):
    devices = mesh.devices
    split = Mesh(
        devices.reshape(4, devices.shape[0] // 8, 2, 4, devices.shape[1] // 4),
        ("far", "near", "core", "x", "y"),
    )
    spec = P(("far", "near", "core"), ("x", "y"))
    return jax.shard_map(
        on_device, mesh=split, in_specs=(spec,) * 4, out_specs=(spec,) * 3, check_vma=False
    )
```
